256 devices in a mesh: row: 16 (over z, y_hi), col: 16 (over y_lo, x, core).
Axes of the slice: x: 4, y: 4 (y_hi: 2, y_lo: 2; y = y_hi * 2 + y_lo), z: 8, core: 2. Of those that a mesh axis runs over, the one named last changes fastest.
Arguments:
- basis_values: bfloat16 [4, 8192, 16384], P(None, 'row', 'col'), may hold values from -6 to 6
- density: float32 [8192, 2560], P('row'), may hold values from -1 to 1, as said below
- screen: int32 [64, 128], P('row', 'col'), may hold values 0 or 1
- atom_of_block: int32 [128], P('col'), may hold values from 0 to 63
- atom_factor: float32 [64], replicated, may hold values from 0.5 to 2
- quad_weight: float32 [16384], P('col'), may hold values from 0.5 to 2
- core_density: float32 [16384], P('col'), may hold values from 0.3 to 1
Outputs:
- xc_matrix: float32 [8192, 1536], P(('row', 'col'))
The draws below stay inside these ranges and needn't reach their ends.
Inputs may be any that keep to these rules, and one draw needn't show every extreme that they name: The density matrix is symmetric. Column block k of a row (k from 0 to 4, 512 columns each) holds the row's entries with the basis block k - 2 places further along the closed chain of 16 blocks; all other entries are zero.
All inputs are finite; a program needn't handle non-finite values. No bound on the sum of `screen` on one device may be relied on, other than what follows from the above.
Results may differ from the reference program's by a relative error of at most 0.0014.
Values may be sent and summed in bfloat16 or wider, within the bound.
A program may use at most 64 MiB of HBM per device.

```python
import math
import jax
import jax.numpy as jnp
from jax import lax

BD = 512
GD = 1024
BAND = 5
SB = 128
GB = 128
ATOMS = 64
NB = 8192
NGP = 16384
N_COL = 16


def draw_density(key, part):
    blocks = NB // BD
    reach = BAND // 2
    key_off = jax.random.fold_in(key, 11)
    key_diagonal = jax.random.fold_in(key, 12)
    random_part = jnp.clip(jax.random.normal(key_off, (blocks, BD, BAND, BD), jnp.float32), -3.0, 3.0)
    diagonal = jax.random.uniform(key_diagonal, (NB,), jnp.float32, 0.5, 1.5)
    pieces = []
    for column in range(BAND):
        mirror = jnp.roll(random_part[:, :, BAND - 1 - column, :], -(column - reach), axis=0)
        pieces.append(0.5 * (random_part[:, :, column, :] + jnp.swapaxes(mirror, 1, 2)))
    banded = jnp.stack(pieces, axis=2)
    off_scale = 0.43 / jnp.sqrt(jnp.float32(NB * BAND * BD))
    banded = off_scale * banded
    identity = jnp.eye(BD, dtype=jnp.float32)
    diagonal_part = diagonal.reshape(blocks, BD)[:, :, None] * identity[None, :, :] / NB
    banded = banded.at[:, :, reach, :].add(diagonal_part)
    return banded.reshape(NB, BAND * BD).astype(jnp.float32)


def touch_ends(result, own_key, smallest, high):
    index_at = [jax.random.randint(jax.random.fold_in(own_key, axis), (), 0, length) for axis, length in enumerate(result.shape)]
    main_axis = result.shape.index(max(result.shape))
    neighbour = index_at[:main_axis] + [(index_at[main_axis] + 1) % result.shape[main_axis]] + index_at[main_axis + 1:]
    return result.at[tuple(index_at)].set(smallest).at[tuple(neighbour)].set(high)


def block_levels(key, dims, cuts, smallest, largest):
    factor_of, own = 1.0, jax.random.fold_in(key, 6)
    for position, parts in cuts:
        steps = jnp.exp(jax.random.uniform(jax.random.fold_in(own, position), (parts,), jnp.float32, smallest / len(cuts), largest / len(cuts)))
        factor_of = factor_of * jnp.repeat(steps, dims[position] // parts).reshape([-1 if axis == position else 1 for axis in range(len(dims))])
    return factor_of


def noise(key, dims, scale, limit, shards=(), kind=jnp.bfloat16):
    result = jax.random.normal(key, dims, jnp.float32) * scale
    if len(shards) > 0:
        result = block_levels(key, dims, shards, -0.22, 0.18) * result
    return jnp.clip(result, min=-limit, max=limit).astype(kind)


def setup_inputs(seed: int = 0) -> dict:
    key_of = jax.random.split(jax.random.key(seed), 8)
    return {
        "basis_values": noise(key_of[0], (4, NB, NGP), 1.0, 6.0, ((1, 16), (2, 16))),
        "density": draw_density(jax.random.fold_in(key_of[7], 71), 0),
        "screen": touch_ends((jax.random.randint(key_of[2], (NB // SB, NGP // GB), 0, 4) < 3).astype(jnp.int32), jax.random.fold_in(key_of[2], 1), 0, 1),
        "atom_of_block": touch_ends(jax.random.randint(key_of[3], (NGP // GB,), 0, ATOMS), jax.random.fold_in(key_of[3], 1), 0, ATOMS - 1).astype(jnp.int32),
        "atom_factor": jnp.clip(jnp.exp(jax.random.uniform(key_of[4], (ATOMS,), jnp.float32, math.log(0.5), math.log(2.0))), 0.5, 2.0),
        "quad_weight": jnp.clip(jnp.exp(math.log(2.0) - 1.3862944 * jax.random.uniform(key_of[5], (NGP,), jnp.float32) ** block_levels(key_of[5], (NGP,), ((0, 16),), -0.2, 0.2)), 0.5, 2.0),
        "core_density": jnp.clip(jnp.exp(math.log(1.0) - 1.2039728 * jax.random.uniform(key_of[6], (NGP,), jnp.float32) ** block_levels(key_of[6], (NGP,), ((0, 16),), -0.2, 0.2)), 0.3, 1.0),
    }


KAPPA_VALUE = 0.804
MU_VALUE = 0.22
SLATER_COEF = 0.7386

def energy_density(density_in, squared_in, core):
    regular = jnp.sqrt(density_in * density_in + core * core)
    reduced = squared_in * regular ** (-8.0 / 3.0)
    enhance = 1.0 + KAPPA_VALUE - KAPPA_VALUE / (1.0 + MU_VALUE * reduced / KAPPA_VALUE)
    return -SLATER_COEF * regular ** (4.0 / 3.0) * enhance

def potentials(density_in, squared_in, core):

    def total_energy(first_arg, second_arg):
        return jnp.sum(energy_density(first_arg, second_arg, core))
    return jax.grad(total_energy, argnums=(0, 1))(density_in, squared_in)

def reference(basis_values, density, screen, atom_of_block, atom_factor, quad_weight, core_density):
    blocks = NB // BD
    reach = BAND // 2
    banded = density.reshape(blocks, BD, BAND, BD)
    factors = atom_factor[atom_of_block]
    per_block = GD // GB

    def grid_block(totals, index):
        first_point = index * GD
        basis = lax.dynamic_slice_in_dim(basis_values, first_point, GD, 2)
        keeper = lax.dynamic_slice_in_dim(screen, index * per_block, per_block, 1)
        masked = (basis.reshape(4, NB // SB, SB, per_block, GB) * keeper.astype(basis.dtype)[None, :, None, :, None]).reshape(4, NB, GD)
        value32 = masked[0].astype(jnp.float32).reshape(blocks, BD, GD)
        applied = jnp.zeros((blocks, BD, GD), jnp.float32)
        for column in range(BAND):
            applied = applied + jnp.einsum('rij,rjg->rig', banded[:, :, column, :], jnp.roll(value32, -(column - reach), axis=0), precision=lax.Precision.HIGHEST)
        applied = applied.reshape(NB, GD)
        masked32 = masked.astype(jnp.float32)
        sums = jnp.einsum('cmg,mg->cg', masked32, applied, precision=lax.Precision.HIGHEST)
        point_density = sums[0]
        gradient = 2.0 * sums[1:]
        squared = lax.optimization_barrier(jnp.sum(gradient * gradient, axis=0))
        block_factor = lax.dynamic_slice_in_dim(factors, index * per_block, per_block, 0)
        quad = lax.dynamic_slice_in_dim(quad_weight, first_point, GD, 0)
        weights = (quad.reshape(per_block, GB) * block_factor[:, None]).reshape(GD) / math.sqrt(NGP)
        core = lax.dynamic_slice_in_dim(core_density, first_point, GD, 0)
        density_pot, gradient_pot = potentials(point_density, squared, core)
        scalar_part = 0.5 * weights * density_pot
        vector_part = 2.0 * weights * gradient_pot * gradient
        half_pot = (scalar_part * masked32[0] + lax.optimization_barrier(jnp.sum(vector_part[:, None, :] * masked32[1:], axis=0))).astype(jnp.bfloat16)
        half32 = half_pot.astype(jnp.float32).reshape(blocks, BD, GD)
        pieces = []
        for column in range(reach + 1):
            first_term = jnp.einsum('rig,rjg->rij', half32, jnp.roll(value32, -column, axis=0), precision=lax.Precision.HIGHEST)
            second_term = jnp.einsum('rig,rjg->rij', value32, jnp.roll(half32, -column, axis=0), precision=lax.Precision.HIGHEST)
            pieces.append(first_term + second_term)
        return (totals + jnp.stack(pieces, axis=2), None)
    start_totals = jnp.zeros((blocks, BD, reach + 1, BD), jnp.float32)
    totals, ignored = lax.scan(grid_block, start_totals, jnp.arange(N_COL, dtype=jnp.int32))
    return totals.reshape(NB, (reach + 1) * BD)
```

```python
import functools
import math

import jax
import jax.numpy as jnp
from jax import lax
from jax.experimental import pallas as pl
from jax.experimental.pallas import tpu as pltpu
from jax.sharding import PartitionSpec as P

F32, BF16 = jnp.float32, jnp.bfloat16
MESH = pl.DeviceIdType.MESH
BAND = 5
KAPPA_VALUE = 0.804
MU_VALUE = 0.22
SLATER_COEF = 0.7386

TILE = 128
CHUNK = 256
X_CHIPS, Y_LOW, CORES, PLANES = 4, 2, 2, 8


def potentials(point, squared, core):
    t_square = point * point + core * core
    log_t = 0.5 * jnp.log(t_square)
    reduced = squared * jnp.exp((-8.0 / 3.0) * log_t)
    inverse = 1.0 / (1.0 + (MU_VALUE / KAPPA_VALUE) * reduced)
    enhance = 1.0 + KAPPA_VALUE - KAPPA_VALUE * inverse
    slope = MU_VALUE * inverse * inverse
    slope_reduced = MU_VALUE * (reduced * inverse) * inverse
    along_t = -SLATER_COEF * jnp.exp((1.0 / 3.0) * log_t) * ((4.0 / 3.0) * enhance - (8.0 / 3.0) * slope_reduced)
    density_pot = along_t * (point * jnp.exp(-log_t))
    gradient_pot = -SLATER_COEF * slope * jnp.exp((-4.0 / 3.0) * log_t)
    return density_pot, gradient_pot


def kernel(
    basis, dens, screen, atom, factor, quad, core_dens, out,
    raw0, comps, dens32, dens_cat, phi, applied, half, acc, part_a, part_b, sum_a, coef,
    core_recv, send_a, send_b, own_a, own_b, recv_a, recv_b, fin, fin_recv,
    raw_sem, comp_sem, dens_sem, phi_send, phi_recv, pa_send, pa_recv, pb_send, pb_recv,
    c_send, c_recv, ra_send, ra_recv, rb_send, rb_recv, f_send, f_recv,
):
    rows = basis.shape[1]
    points = basis.shape[2]
    steps = points // CHUNK
    blocks = CHUNK // TILE
    row_tiles = rows // TILE
    row, col = lax.axis_index("row"), lax.axis_index("col")
    plane, side = row // 2, row % 2
    low, chip_x, core = col // (X_CHIPS * CORES), (col // CORES) % X_CHIPS, col % CORES
    way = 1 - 2 * side

    def at_row(new_plane, new_side):
        return {"row": lax.rem(new_plane + PLANES, PLANES) * 2 + new_side, "col": col}

    def at_chip(dy, dx):
        return {"row": row, "col": (((low + dy) % Y_LOW) * X_CHIPS + (chip_x + dx) % X_CHIPS) * CORES + core}

    paired = plane + 1 - 2 * (plane % 2)
    partner = at_row(plane, 1 - side)
    far, near = at_row(plane + way, side), at_row(plane - way, side)
    odd = at_row(plane - way, 1 - side)
    group_a = [partner, at_row(paired, side), at_row(paired, 1 - side)]
    group_b = [at_row(plane + 2, side), at_row(plane + 4, side), at_row(plane + 6, side)]
    sibling = {"row": row, "col": col + 1 - 2 * core}
    chips = [(dy, dx) for dy in range(Y_LOW) for dx in range(X_CHIPS) if dy or dx]
    chip_ids = [at_chip(dy, dx) for dy, dx in chips]
    behind1 = {"row": lax.rem(row + 15, 16), "col": col}
    behind2 = {"row": lax.rem(row + 14, 16), "col": col}

    def raw_copy(j):
        return pltpu.make_async_copy(basis.at[0, :, pl.ds(j * CHUNK, CHUNK)], raw0.at[j], raw_sem.at[j])

    def comp_copy(j):
        return pltpu.make_async_copy(basis.at[pl.ds(1, 3), :, pl.ds(j * CHUNK, CHUNK)], comps.at[j], comp_sem.at[j])

    dens_copy = pltpu.make_async_copy(dens, dens32, dens_sem)
    for j in range(steps):
        raw_copy(j).start()
    dens_copy.start()
    for j in range(steps):
        comp_copy(j).start()

    barrier = pltpu.get_barrier_semaphore()
    peers = [partner, far, near, odd, group_a[2], *group_b, sibling, *chip_ids]
    for peer in peers:
        pl.semaphore_signal(barrier, inc=1, device_id=peer, device_id_type=MESH)

    def remote(src, dst, send, recv, device):
        return pltpu.make_async_remote_copy(
            src_ref=src, dst_ref=dst, send_sem=send, recv_sem=recv, device_id=device, device_id_type=MESH
        )

    def own_sends(j):
        return [
            remote(phi.at[j, 2], phi.at[j, 2 - way], phi_send.at[0, j], phi_recv.at[0, j], partner),
            remote(phi.at[j, 2], phi.at[j, 2 - 2 * way], phi_send.at[1, j], phi_recv.at[1, j], far),
            remote(phi.at[j, 2], phi.at[j, 2 + 2 * way], phi_send.at[2, j], phi_recv.at[2, j], near),
        ]

    def own_recvs(j):
        return [
            remote(phi.at[j, 2], phi.at[j, 2 + way], phi_send.at[0, j], phi_recv.at[0, j], partner),
            remote(phi.at[j, 2], phi.at[j, 2 - 2 * way], phi_send.at[1, j], phi_recv.at[1, j], near),
            remote(phi.at[j, 2], phi.at[j, 2 + 2 * way], phi_send.at[2, j], phi_recv.at[2, j], far),
        ]

    def forward(j):
        even = j % 2 == 0
        src = jnp.where(even, 2 + way, 2 + 2 * way)
        dst = jnp.where(even, 2 - way, 2 + way)
        target = {"row": jnp.where(even, far["row"], partner["row"]), "col": col}
        return remote(phi.at[j, src], phi.at[j, dst], phi_send.at[3, j], phi_recv.at[3, j], target)

    def forward_recv(j):
        return remote(phi.at[j, 2], phi.at[j, 2 - way], phi_send.at[3, j], phi_recv.at[3, j], partner)

    def keep(i, j, b):
        return screen[i, j * blocks + b].astype(F32)

    def tile(i, b):
        return slice(i * TILE, (i + 1) * TILE), slice(b * TILE, (b + 1) * TILE)

    def mask_own(j):
        for i in range(row_tiles):
            for b in range(blocks):
                r, c = tile(i, b)
                phi[j, 2, r, c] = (raw0[j, r, c].astype(F32) * keep(i, j, b)).astype(BF16)

    raw_copy(0).wait()
    mask_own(0)
    pl.semaphore_wait(barrier, len(peers))
    for copy in own_sends(0):
        copy.start()
    for j in range(1, steps):
        raw_copy(j).wait()
        mask_own(j)
        if j == 1:
            for copy in own_sends(1):
                copy.start()

    dens_copy.wait()

    @pl.loop(0, rows // 32)
    def _(i):
        at = pl.multiple_of(i * 32, 32)
        whole = dens32[pl.ds(at, 32), :]
        high = whole.astype(BF16)
        dens_cat[pl.ds(at, 32), :] = high
        dens_cat[pl.ds(rows + at, 32), :] = (whole - high.astype(F32)).astype(BF16)

    acc[...] = jnp.zeros_like(acc)

    def a_copies(j):
        return [
            remote(part_a.at[j, 3], part_a.at[j, i], pa_send.at[j, i], pa_recv.at[j, i], peer)
            for i, peer in enumerate(group_a)
        ]

    def b_copies(j):
        return [
            remote(sum_a.at[j], part_b.at[j, i], pb_send.at[j, i], pb_recv.at[j, i], peer)
            for i, peer in enumerate(group_b)
        ]

    def density_step(j):
        applied[...] = jnp.dot(
            dens_cat[...], phi[j].reshape(BAND * rows, CHUNK), preferred_element_type=F32
        )
        for b in range(blocks):
            sums = [jnp.zeros((1, TILE), F32)] * 4
            for i in range(row_tiles):
                r, c = tile(i, b)
                low_rows = slice(rows + i * TILE, rows + (i + 1) * TILE)
                mine = (applied[r, c] + applied[low_rows, c]) * keep(i, j, b)
                sums[0] = sums[0] + jnp.sum(mine * phi[j, 2, r, c].astype(F32), axis=0, keepdims=True)
                for d in range(3):
                    sums[d + 1] = sums[d + 1] + jnp.sum(mine * comps[j, d, r, c].astype(F32), axis=0, keepdims=True)
            for d in range(4):
                part_a[j, 3, d * blocks + b : d * blocks + b + 1, :] = sums[d]

    def potential_step(j):
        total = sum_a[j]
        for i in range(3):
            total = total + part_b[j, i]
        point = total[0:blocks]
        grads = [2.0 * total[d * blocks : (d + 1) * blocks] for d in (1, 2, 3)]
        squared = grads[0] * grads[0] + grads[1] * grads[1] + grads[2] * grads[2]
        at = j * blocks
        lines = [quad[pl.ds(at + b, 1), :] * factor[atom[at + b]] for b in range(blocks)]
        weights = jnp.concatenate(lines, axis=0) * (1.0 / math.sqrt(points * 16))
        density_pot, gradient_pot = potentials(point, squared, core_dens[pl.ds(at, blocks), :])
        coef[0:blocks, :] = 0.5 * weights * density_pot
        for d in range(3):
            coef[(d + 1) * blocks : (d + 2) * blocks, :] = 2.0 * weights * gradient_pot * grads[d]
        for b in range(blocks):
            factors = [coef[d * blocks + b : d * blocks + b + 1, :] for d in range(4)]
            for i in range(row_tiles):
                r, c = tile(i, b)
                value = factors[0] * phi[j, 2, r, c].astype(F32)
                rest = factors[1] * comps[j, 0, r, c].astype(F32)
                for d in range(1, 3):
                    rest = rest + factors[d + 1] * comps[j, d, r, c].astype(F32)
                half[r, c] = ((value + rest) * keep(i, j, b)).astype(BF16)

    def matrix_step(j):
        def contract(left, right):
            return lax.dot_general(left, right, (((1,), (1,)), ((), ())), preferred_element_type=F32)

        shape = acc.shape[1:]
        pot = half[...]
        acc[0] += contract(phi[j, 0], pot).reshape(shape)
        acc[1] += contract(phi[j, 1], pot).reshape(shape)
        acc[2] += (contract(pot, phi[j, 2]) + contract(phi[j, 2], pot)).reshape(shape)
        acc[3] += contract(pot, phi[j, 3]).reshape(shape)
        acc[4] += contract(pot, phi[j, 4]).reshape(shape)

    def wait_direct(j):
        partner_in, near_in, far_in = own_recvs(j)
        partner_in.wait_recv()
        far_in.wait_recv()

    wait_direct(0)
    forward(0).start()

    @pl.loop(0, steps + 1)
    def _(t):
        @pl.when(t + 1 < steps)
        def _():
            wait_direct(t + 1)
            forward(t + 1).start()

        @pl.when(t + 2 < steps)
        def _():
            for copy in own_sends(t + 2):
                copy.start()

        @pl.when(t >= 1)
        def _():
            j = t - 1
            for copy in a_copies(j):
                copy.wait_recv()
            sum_a[j] = (part_a[j, 3] + part_a[j, 0]) + (part_a[j, 1] + part_a[j, 2])
            for copy in b_copies(j):
                copy.start()

        @pl.when(t < steps)
        def _():
            own_recvs(t)[1].wait_recv()
            forward_recv(t).wait_recv()
            comp_copy(t).wait()
            density_step(t)
            for copy in a_copies(t):
                copy.start()

        @pl.when(t >= 1)
        def _():
            j = t - 1
            for copy in b_copies(j):
                copy.wait_recv()
            potential_step(j)
            matrix_step(j)

    def core_copy(k):
        return remote(acc.at[k, :, 1 - core], core_recv.at[k], c_send.at[k], c_recv.at[k], sibling)

    for k in range(BAND):
        core_copy(k).start()
    mine = low * X_CHIPS + chip_x

    def fold(k, send, own, place):
        core_copy(k).wait_recv()
        total = acc[k, :, core] + core_recv[k]
        acc[k, :, core] = total
        send[:, place] = total.astype(BF16)
        own[place] = acc[k, mine, core]

    def chip_copies(send, recv, ssem, rsem):
        return [
            remote(send.at[((low + dy) % Y_LOW) * X_CHIPS + (chip_x + dx) % X_CHIPS], recv.at[i], ssem.at[i], rsem.at[i], peer)
            for i, ((dy, dx), peer) in enumerate(zip(chips, chip_ids))
        ]

    fold(0, send_a, own_a, 0)
    fold(1, send_a, own_a, 1)
    copies_a = chip_copies(send_a, recv_a, ra_send, ra_recv)
    for copy in copies_a:
        copy.start()
    for k in (2, 3, 4):
        fold(k, send_b, own_b, k - 2)
    copies_b = chip_copies(send_b, recv_b, rb_send, rb_recv)
    for copy in copies_b:
        copy.start()

    for copy in copies_a:
        copy.wait_recv()
    total = own_a[...]
    for i in range(len(chips)):
        total = total + recv_a[i].astype(F32)
    fin[...] = total
    last = [
        remote(fin.at[0], fin_recv.at[0], f_send.at[0], f_recv.at[0], behind2),
        remote(fin.at[1], fin_recv.at[1], f_send.at[1], f_recv.at[1], behind1),
    ]
    for copy in last:
        copy.start()
    for copy in copies_b:
        copy.wait_recv()
    for k in range(3):
        total = own_b[k]
        for i in range(len(chips)):
            total = total + recv_b[i, k].astype(F32)
        if k:
            last[2 - k].wait_recv()
            total = total + fin_recv[2 - k]
        out[:, k * rows : (k + 1) * rows] = total

    for j in range(steps):
        for copy in own_sends(j):
            copy.wait_send()
        forward(j).wait_send()
        for copy in a_copies(j) + b_copies(j):
            copy.wait_send()
    for k in range(BAND):
        core_copy(k).wait_send()
    for copy in copies_a + copies_b + last:
        copy.wait_send()


def body(basis_values, density, screen, atom_of_block, atom_factor, quad_weight, core_density):
    rows, points = basis_values.shape[1:]
    steps = points // CHUNK
    piece = rows // 16
    dma = pltpu.SemaphoreType.DMA
    vmem, smem, hbm = (pl.BlockSpec(memory_space=s) for s in (pltpu.VMEM, pltpu.SMEM, pl.ANY))
    flat = 4 * CHUNK // TILE
    return pl.pallas_call(
        kernel,
        out_shape=jax.ShapeDtypeStruct((piece, 3 * rows), F32),
        in_specs=[hbm, hbm, smem, smem, smem, vmem, vmem],
        out_specs=vmem,
        scratch_shapes=[
            pltpu.VMEM((steps, rows, CHUNK), BF16),
            pltpu.VMEM((steps, 3, rows, CHUNK), BF16),
            pltpu.VMEM((rows, BAND * rows), F32),
            pltpu.VMEM((2 * rows, BAND * rows), BF16),
            pltpu.VMEM((steps, BAND, rows, CHUNK), BF16),
            pltpu.VMEM((2 * rows, CHUNK), F32),
            pltpu.VMEM((rows, CHUNK), BF16),
            pltpu.VMEM((BAND, 8, CORES, piece, rows), F32),
            pltpu.VMEM((steps, 4, flat, TILE), F32),
            pltpu.VMEM((steps, 3, flat, TILE), F32),
            pltpu.VMEM((steps, flat, TILE), F32),
            pltpu.VMEM((flat, TILE), F32),
            pltpu.VMEM((BAND, 8, piece, rows), F32),
            pltpu.VMEM((8, 2, piece, rows), BF16),
            pltpu.VMEM((8, 3, piece, rows), BF16),
            pltpu.VMEM((2, piece, rows), F32),
            pltpu.VMEM((3, piece, rows), F32),
            pltpu.VMEM((7, 2, piece, rows), BF16),
            pltpu.VMEM((7, 3, piece, rows), BF16),
            pltpu.VMEM((2, piece, rows), F32),
            pltpu.VMEM((2, piece, rows), F32),
            dma((steps,)), dma((steps,)), dma,
            dma((4, steps)), dma((4, steps)),
            dma((steps, 3)), dma((steps, 3)), dma((steps, 3)), dma((steps, 3)),
            dma((BAND,)), dma((BAND,)),
            dma((7,)), dma((7,)), dma((7,)), dma((7,)),
            dma((2,)), dma((2,)),
        ],
        compiler_params=pltpu.CompilerParams(
            collective_id=0, has_side_effects=True, vmem_limit_bytes=56 << 20
        ),
        name="xc_matrix",
    )(
        basis_values, density, screen, atom_of_block, atom_factor,
        quad_weight.reshape(-1, TILE), core_density.reshape(-1, TILE),
    )


def solution(mesh):
    in_specs = (
        P(None, "row", "col"),
        P("row", None),
        P("row", "col"),
        P("col"),
        P(),
        P("col"),
        P("col"),
    )
    out_specs = P(("row", "col"), None)
    return jax.shard_map(body, mesh=mesh, in_specs=in_specs, out_specs=out_specs, check_vma=False)
```

```python
import functools
import math

import jax
import jax.numpy as jnp
from jax import lax
from jax.experimental import pallas as pl
from jax.experimental.pallas import tpu as pltpu
from jax.sharding import PartitionSpec as P

F32, BF16 = jnp.float32, jnp.bfloat16
MESH = pl.DeviceIdType.MESH
BAND = 5
KAPPA_VALUE = 0.804
MU_VALUE = 0.22
SLATER_COEF = 0.7386

TILE = 128
CHUNK = 256
X_CHIPS, Y_LOW, CORES, PLANES = 4, 2, 2, 8
DEPTH = 3
LEAD = 1
LAG_A, LAG_B = 1, 2


def potentials(point, squared, core):
    t_square = point * point + core * core
    log_t = 0.5 * jnp.log(t_square)
    reduced = squared * jnp.exp((-8.0 / 3.0) * log_t)
    inverse = 1.0 / (1.0 + (MU_VALUE / KAPPA_VALUE) * reduced)
    enhance = 1.0 + KAPPA_VALUE - KAPPA_VALUE * inverse
    slope = MU_VALUE * inverse * inverse
    slope_reduced = MU_VALUE * (reduced * inverse) * inverse
    along_t = -SLATER_COEF * jnp.exp((1.0 / 3.0) * log_t) * ((4.0 / 3.0) * enhance - (8.0 / 3.0) * slope_reduced)
    density_pot = along_t * (point * jnp.exp(-log_t))
    gradient_pot = -SLATER_COEF * slope * jnp.exp((-4.0 / 3.0) * log_t)
    return density_pot, gradient_pot


def kernel(
    basis, dens, screen, atom, factor, quad, core_dens, out,
    raw0, comps, dens32, dens_cat, phi, phi_sib, applied, half, half_sib, acc, part_a, part_b, sum_a, coef,
    send, own, recv, fin, fin_recv,
    raw_sem, comp_sem, dens_sem, phi_send, phi_recv, pa_send, pa_recv, pb_send, pb_recv,
    c_send, c_recv, r_send, r_recv, f_send, f_recv,
):
    rows = basis.shape[1]
    points = basis.shape[2]
    steps = points // CHUNK
    blocks = CHUNK // TILE
    row_tiles = rows // TILE
    row, col = lax.axis_index("row"), lax.axis_index("col")
    plane, side = row // 2, row % 2
    low, chip_x, core = col // (X_CHIPS * CORES), (col // CORES) % X_CHIPS, col % CORES
    way = 1 - 2 * side

    def at_row(new_plane, new_side):
        return {"row": lax.rem(new_plane + PLANES, PLANES) * 2 + new_side, "col": col}

    def at_chip(dy, dx):
        return {"row": row, "col": (((low + dy) % Y_LOW) * X_CHIPS + (chip_x + dx) % X_CHIPS) * CORES + core}

    paired = plane + 1 - 2 * (plane % 2)
    partner = at_row(plane, 1 - side)
    far, near = at_row(plane + way, side), at_row(plane - way, side)
    odd = at_row(plane - way, 1 - side)
    group_a = [partner, at_row(paired, side), at_row(paired, 1 - side)]
    group_b = [at_row(plane + 2, side), at_row(plane + 4, side), at_row(plane + 6, side)]
    sibling = {"row": row, "col": col + 1 - 2 * core}
    chips = [(dy, dx) for dy in range(Y_LOW) for dx in range(X_CHIPS) if dy or dx]
    chip_ids = [at_chip(dy, dx) for dy, dx in chips]
    behind1 = {"row": lax.rem(row + 15, 16), "col": col}
    behind2 = {"row": lax.rem(row + 14, 16), "col": col}

    def raw_copy(j):
        return pltpu.make_async_copy(basis.at[0, :, pl.ds(j * CHUNK, CHUNK)], raw0.at[j], raw_sem.at[j])

    def comp_copy(j):
        return pltpu.make_async_copy(basis.at[pl.ds(1, 3), :, pl.ds(j * CHUNK, CHUNK)], comps.at[j], comp_sem.at[j])

    dens_copy = pltpu.make_async_copy(dens, dens32, dens_sem)
    for j in range(steps):
        raw_copy(j).start()
    dens_copy.start()
    for j in range(steps):
        comp_copy(j).start()

    barrier = pltpu.get_barrier_semaphore()
    peers = [partner, far, near, odd, group_a[2], *group_b, sibling, *chip_ids]
    for peer in peers:
        pl.semaphore_signal(barrier, inc=1, device_id=peer, device_id_type=MESH)

    def remote(src, dst, send, recv, device):
        return pltpu.make_async_remote_copy(
            src_ref=src, dst_ref=dst, send_sem=send, recv_sem=recv, device_id=device, device_id_type=MESH
        )

    def half_block(j, k, h):
        return phi.at[j, k, pl.ds(4 * h, 4)]

    def block_copy(j, route, src, dst, h, device):
        return remote(
            half_block(j, src, h), half_block(j, dst, h), phi_send.at[route, h, j], phi_recv.at[route, h, j], device
        )

    def own_sends(j):
        order = [(0, 0), (1, 1), (2, 0), (0, 1), (1, 0), (2, 1)]
        place = [(2 - way, partner), (2 - 2 * way, far), (2 + 2 * way, near)]
        return [block_copy(j, route, 2, place[route][0], h, place[route][1]) for route, h in order]

    def block_recv(j, route, h):
        place = [(2 + way, partner), (2 - 2 * way, near), (2 + 2 * way, far), (2 - way, partner)]
        return block_copy(j, route, 2, place[route][0], h, place[route][1])

    def forwards(j):
        return [
            block_copy(j, 3, 2 + way, 2 - way, 0, far),
            block_copy(j, 3, 2 + 2 * way, 2 + way, 1, partner),
        ]

    def keep(i, j, b):
        return screen[i, j * blocks + b].astype(F32)

    def tile(i, b):
        return slice(i * TILE, (i + 1) * TILE), slice(b * TILE, (b + 1) * TILE)

    piece = rows // (8 * CORES)
    tile_shape = (TILE // (CORES * piece), CORES, piece, TILE)

    def folded(i, b):
        wide = tile_shape[0]
        return slice(i * wide, (i + 1) * wide), slice(None), slice(None), slice(b * TILE, (b + 1) * TILE)

    def phi_tile(j, i, b):
        return phi[(j, 2, *folded(i, b))].reshape(TILE, TILE).astype(F32)

    def mask_own(j):
        for i in range(row_tiles):
            for b in range(blocks):
                r, c = tile(i, b)
                value = (raw0[j, r, c].astype(F32) * keep(i, j, b)).astype(BF16)
                phi[(j, 2, *folded(i, b))] = value.reshape(tile_shape)

    raw_copy(0).wait()
    mask_own(0)
    pl.semaphore_wait(barrier, len(peers))
    for copy in own_sends(0):
        copy.start()
    for j in range(1, steps):
        raw_copy(j).wait()
        mask_own(j)
        if j < DEPTH:
            for copy in own_sends(j):
                copy.start()

    dens_copy.wait()

    @pl.loop(0, rows // 32)
    def _(i):
        at = pl.multiple_of(i * 32, 32)
        whole = dens32[pl.ds(at, 32), :]
        high = whole.astype(BF16)
        dens_cat[pl.ds(at, 32), :] = high
        dens_cat[pl.ds(rows + at, 32), :] = (whole - high.astype(F32)).astype(BF16)

    acc[...] = jnp.zeros_like(acc)

    def a_copies(j):
        return [
            remote(part_a.at[j, 3], part_a.at[j, i], pa_send.at[j, i], pa_recv.at[j, i], peer)
            for i, peer in enumerate(group_a)
        ]

    def b_copies(j):
        return [
            remote(sum_a.at[j], part_b.at[j, i], pb_send.at[j, i], pb_recv.at[j, i], peer)
            for i, peer in enumerate(group_b)
        ]

    def density_step(j):
        applied[...] = jnp.dot(
            dens_cat[...], phi[j].reshape(BAND * rows, CHUNK), preferred_element_type=F32
        )
        for b in range(blocks):
            sums = [jnp.zeros((1, TILE), F32)] * 4
            for i in range(row_tiles):
                r, c = tile(i, b)
                low_rows = slice(rows + i * TILE, rows + (i + 1) * TILE)
                mine = (applied[r, c] + applied[low_rows, c]) * keep(i, j, b)
                sums[0] = sums[0] + jnp.sum(mine * phi_tile(j, i, b), axis=0, keepdims=True)
                for d in range(3):
                    sums[d + 1] = sums[d + 1] + jnp.sum(mine * comps[j, d, r, c].astype(F32), axis=0, keepdims=True)
            for d in range(4):
                part_a[j, 3, d * blocks + b : d * blocks + b + 1, :] = sums[d]

    def potential_step(j):
        total = sum_a[j]
        for i in range(3):
            total = total + part_b[j, i]
        point = total[0:blocks]
        grads = [2.0 * total[d * blocks : (d + 1) * blocks] for d in (1, 2, 3)]
        squared = grads[0] * grads[0] + grads[1] * grads[1] + grads[2] * grads[2]
        at = j * blocks
        lines = [quad[pl.ds(at + b, 1), :] * factor[atom[at + b]] for b in range(blocks)]
        weights = jnp.concatenate(lines, axis=0) * (1.0 / math.sqrt(points * 16))
        density_pot, gradient_pot = potentials(point, squared, core_dens[pl.ds(at, blocks), :])
        coef[0:blocks, :] = 0.5 * weights * density_pot
        for d in range(3):
            coef[(d + 1) * blocks : (d + 2) * blocks, :] = 2.0 * weights * gradient_pot * grads[d]
        for b in range(blocks):
            factors = [coef[d * blocks + b : d * blocks + b + 1, :] for d in range(4)]
            for i in range(row_tiles):
                r, c = tile(i, b)
                value = factors[0] * phi_tile(j, i, b)
                rest = factors[1] * comps[j, 0, r, c].astype(F32)
                for d in range(1, 3):
                    rest = rest + factors[d + 1] * comps[j, d, r, c].astype(F32)
                pot = ((value + rest) * keep(i, j, b)).astype(BF16)
                half[(j, *folded(i, b))] = pot.reshape(tile_shape)

    def sibling_blocks(j):
        ahead, other = pl.ds(2, 3), 1 - core
        return [
            remote(phi.at[j, ahead], phi_sib.at[j, ahead], c_send.at[0, j], c_recv.at[0, j], sibling),
            remote(
                phi.at[j, pl.ds(0, 2), :, other], phi_sib.at[j, pl.ds(0, 2), :, other],
                c_send.at[1, j], c_recv.at[1, j], sibling,
            ),
        ]

    def sibling_half(j):
        return remote(half.at[j], half_sib.at[j], c_send.at[2, j], c_recv.at[2, j], sibling)

    def matrix_part(j, block, pot, offsets):
        def contract(left, right):
            return lax.dot_general(left, right, (((1,), (1,)), ((), ())), preferred_element_type=F32)

        own_pot = pot[j, :, core].reshape(rows // CORES, CHUNK)
        all_pot = pot[j].reshape(rows, CHUNK)
        for k in offsets:
            term = 0.0
            if k <= 2:
                term = contract(block[j, k, :, core].reshape(rows // CORES, CHUNK), all_pot)
            if k >= 2:
                term = term + contract(own_pot, block[j, k].reshape(rows, CHUNK))
            acc[k] += term.reshape(acc.shape[1:])

    def pass_on(j):
        first, second = forwards(j)
        block_recv(j, 0, 0).wait_recv()
        first.start()
        block_recv(j, 2, 1).wait_recv()
        second.start()

    for j in range(LEAD):
        pass_on(j)

    @pl.loop(0, steps + LAG_B)
    def _(t):
        @pl.when(t + DEPTH < steps)
        def _():
            for copy in own_sends(t + DEPTH):
                copy.start()

        @pl.when(t + LEAD < steps)
        def _():
            pass_on(t + LEAD)

        @pl.when(t < steps)
        def _():
            for route, h in ((0, 1), (2, 0), (1, 0), (1, 1), (3, 0), (3, 1)):
                block_recv(t, route, h).wait_recv()
            for copy in sibling_blocks(t):
                copy.start()
            comp_copy(t).wait()
            density_step(t)
            for copy in a_copies(t):
                copy.start()

        @pl.when((t >= LAG_A) & (t < steps + LAG_A))
        def _():
            j = t - LAG_A
            for copy in a_copies(j):
                copy.wait_recv()
            sum_a[j] = (part_a[j, 3] + part_a[j, 0]) + (part_a[j, 1] + part_a[j, 2])
            for copy in b_copies(j):
                copy.start()

        @pl.when(t >= LAG_B)
        def _():
            j = t - LAG_B
            for copy in b_copies(j):
                copy.wait_recv()
            potential_step(j)
            sibling_half(j).start()
            matrix_part(j, phi, half, range(BAND))

        @pl.when(t >= LAG_B + 1)
        def _():
            j = t - LAG_B - 1
            for copy in (*sibling_blocks(j), sibling_half(j)):
                copy.wait_recv()
            matrix_part(j, phi_sib, half_sib, range(BAND))

    mine = low * X_CHIPS + chip_x

    def chip_copies(k):
        return [
            remote(
                send.at[k, ((low + dy) % Y_LOW) * X_CHIPS + (chip_x + dx) % X_CHIPS], recv.at[k, i],
                r_send.at[k, i], r_recv.at[k, i], peer,
            )
            for i, ((dy, dx), peer) in enumerate(zip(chips, chip_ids))
        ]

    for copy in (*sibling_blocks(steps - 1), sibling_half(steps - 1)):
        copy.wait_recv()
    for k in range(BAND):
        matrix_part(steps - 1, phi_sib, half_sib, (k,))
        send[k] = acc[k].astype(BF16)
        for copy in chip_copies(k):
            copy.start()
        own[k] = acc[k, mine]

    def collect(k):
        for copy in chip_copies(k):
            copy.wait_recv()
        total = own[k]
        for i in range(len(chips)):
            total = total + recv[k, i].astype(F32)
        return total

    last = [
        remote(fin.at[0], fin_recv.at[0], f_send.at[0], f_recv.at[0], behind2),
        remote(fin.at[1], fin_recv.at[1], f_send.at[1], f_recv.at[1], behind1),
    ]
    for k in range(2):
        fin[k] = collect(k)
        last[k].start()
    totals = [collect(k) for k in (2, 3, 4)]
    out[:, 0:rows] = totals[0]
    for k in (1, 2):
        last[2 - k].wait_recv()
        out[:, k * rows : (k + 1) * rows] = totals[k] + fin_recv[2 - k]

    for j in range(steps):
        for copy in (*own_sends(j), *forwards(j)):
            copy.wait_send()
        for copy in (*a_copies(j), *b_copies(j), *sibling_blocks(j), sibling_half(j)):
            copy.wait_send()
    for k in range(BAND):
        for copy in chip_copies(k):
            copy.wait_send()
    for copy in last:
        copy.wait_send()


def body(basis_values, density, screen, atom_of_block, atom_factor, quad_weight, core_density):
    rows, points = basis_values.shape[1:]
    steps = points // CHUNK
    piece = rows // 16
    dma = pltpu.SemaphoreType.DMA
    vmem, smem, hbm = (pl.BlockSpec(memory_space=s) for s in (pltpu.VMEM, pltpu.SMEM, pl.ANY))
    flat = 4 * CHUNK // TILE
    return pl.pallas_call(
        kernel,
        out_shape=jax.ShapeDtypeStruct((piece, 3 * rows), F32),
        in_specs=[hbm, hbm, smem, smem, smem, vmem, vmem],
        out_specs=vmem,
        scratch_shapes=[
            pltpu.VMEM((steps, rows, CHUNK), BF16),
            pltpu.VMEM((steps, 3, rows, CHUNK), BF16),
            pltpu.VMEM((rows, BAND * rows), F32),
            pltpu.VMEM((2 * rows, BAND * rows), BF16),
            pltpu.VMEM((steps, BAND, 8, CORES, piece, CHUNK), BF16),
            pltpu.VMEM((steps, BAND, 8, CORES, piece, CHUNK), BF16),
            pltpu.VMEM((2 * rows, CHUNK), F32),
            pltpu.VMEM((steps, 8, CORES, piece, CHUNK), BF16),
            pltpu.VMEM((steps, 8, CORES, piece, CHUNK), BF16),
            pltpu.VMEM((BAND, 8, piece, rows), F32),
            pltpu.VMEM((steps, 4, flat, TILE), F32),
            pltpu.VMEM((steps, 3, flat, TILE), F32),
            pltpu.VMEM((steps, flat, TILE), F32),
            pltpu.VMEM((flat, TILE), F32),
            pltpu.VMEM((BAND, 8, piece, rows), BF16),
            pltpu.VMEM((BAND, piece, rows), F32),
            pltpu.VMEM((BAND, 7, piece, rows), BF16),
            pltpu.VMEM((2, piece, rows), F32),
            pltpu.VMEM((2, piece, rows), F32),
            dma((steps,)), dma((steps,)), dma,
            dma((4, 2, steps)), dma((4, 2, steps)),
            dma((steps, 3)), dma((steps, 3)), dma((steps, 3)), dma((steps, 3)),
            dma((3, steps)), dma((3, steps)),
            dma((BAND, 7)), dma((BAND, 7)),
            dma((2,)), dma((2,)),
        ],
        compiler_params=pltpu.CompilerParams(
            collective_id=0, has_side_effects=True, vmem_limit_bytes=56 << 20
        ),
        name="xc_matrix",
    )(
        basis_values, density, screen, atom_of_block, atom_factor,
        quad_weight.reshape(-1, TILE), core_density.reshape(-1, TILE),
    )


def solution(mesh):
    in_specs = (
        P(None, "row", "col"),
        P("row", None),
        P("row", "col"),
        P("col"),
        P(),
        P("col"),
        P("col"),
    )
    out_specs = P(("row", "col"), None)
    return jax.shard_map(body, mesh=mesh, in_specs=in_specs, out_specs=out_specs, check_vma=False)
```

```python
import functools
import math

import jax
import jax.numpy as jnp
from jax import lax
from jax.experimental import pallas as pl
from jax.experimental.pallas import tpu as pltpu
from jax.sharding import PartitionSpec as P

F32, BF16 = jnp.float32, jnp.bfloat16
MESH = pl.DeviceIdType.MESH
BAND = 5
KAPPA_VALUE = 0.804
MU_VALUE = 0.22
SLATER_COEF = 0.7386

TILE = 128
CHUNK = 256
X_FIRST = (0, 2, 4)
X_CHIPS, Y_LOW, CORES, PLANES = 4, 2, 2, 8
DEPTH = 3
LEAD = 1
LAG_A, LAG_B = 1, 2


def potentials(point, squared, core):
    t_square = point * point + core * core
    log_t = 0.5 * jnp.log(t_square)
    reduced = squared * jnp.exp((-8.0 / 3.0) * log_t)
    inverse = 1.0 / (1.0 + (MU_VALUE / KAPPA_VALUE) * reduced)
    enhance = 1.0 + KAPPA_VALUE - KAPPA_VALUE * inverse
    slope = MU_VALUE * inverse * inverse
    slope_reduced = MU_VALUE * (reduced * inverse) * inverse
    along_t = -SLATER_COEF * jnp.exp((1.0 / 3.0) * log_t) * ((4.0 / 3.0) * enhance - (8.0 / 3.0) * slope_reduced)
    density_pot = along_t * (point * jnp.exp(-log_t))
    gradient_pot = -SLATER_COEF * slope * jnp.exp((-4.0 / 3.0) * log_t)
    return density_pot, gradient_pot


def kernel(
    basis, dens, screen, atom, factor, quad, core_dens, out,
    raw0, comps, dens32, dens_cat, phi, phi_sib, applied, half, half_sib, acc, part_a, part_b, sum_a, coef,
    send, recv_x, recv_y, mid_y, mid_y32, mid_x, got_y, got_y32, got_x, got_x1, own, fin, fin_recv,
    raw_sem, comp_sem, dens_sem, phi_send, phi_recv, pa_send, pa_recv, pb_send, pb_recv,
    c_send, c_recv, r_send, r_recv, m_send, m_recv,
):
    rows = basis.shape[1]
    points = basis.shape[2]
    steps = points // CHUNK
    blocks = CHUNK // TILE
    row_tiles = rows // TILE
    row, col = lax.axis_index("row"), lax.axis_index("col")
    plane, side = row // 2, row % 2
    low, chip_x, core = col // (X_CHIPS * CORES), (col // CORES) % X_CHIPS, col % CORES
    way = 1 - 2 * side

    def at_row(new_plane, new_side):
        return {"row": lax.rem(new_plane + PLANES, PLANES) * 2 + new_side, "col": col}

    def at_chip(dy, dx, offset=0):
        return {"row": lax.rem(row + offset + 16, 16), "col": (((low + dy) % Y_LOW) * X_CHIPS + (chip_x + dx) % X_CHIPS) * CORES + core}

    paired = plane + 1 - 2 * (plane % 2)
    partner = at_row(plane, 1 - side)
    far, near = at_row(plane + way, side), at_row(plane - way, side)
    odd = at_row(plane - way, 1 - side)
    group_a = [partner, at_row(paired, side), at_row(paired, 1 - side)]
    group_b = [at_row(plane + 2, side), at_row(plane + 4, side), at_row(plane + 6, side)]
    sibling = {"row": row, "col": col + 1 - 2 * core}
    across_y = at_chip(1, 0)
    along_x = [at_chip(0, dx) for dx in range(1, X_CHIPS)]
    shifted = [at_chip(1, 0, offset) for offset in (-2, 2)]
    shifted += [at_chip(0, dx, offset) for offset in (-1, 1) for dx in range(1, X_CHIPS)]

    def raw_copy(j):
        return pltpu.make_async_copy(basis.at[0, :, pl.ds(j * CHUNK, CHUNK)], raw0.at[j], raw_sem.at[j])

    def comp_copy(j):
        return pltpu.make_async_copy(basis.at[pl.ds(1, 3), :, pl.ds(j * CHUNK, CHUNK)], comps.at[j], comp_sem.at[j])

    dens_copy = pltpu.make_async_copy(dens, dens32, dens_sem)
    for j in range(steps):
        raw_copy(j).start()
    dens_copy.start()
    for j in range(steps):
        comp_copy(j).start()

    barrier = pltpu.get_barrier_semaphore()
    peers = [partner, far, near, odd, group_a[2], *group_b, sibling, across_y, *along_x, *shifted]
    for peer in peers:
        pl.semaphore_signal(barrier, inc=1, device_id=peer, device_id_type=MESH)

    def remote(src, dst, send, recv, device):
        return pltpu.make_async_remote_copy(
            src_ref=src, dst_ref=dst, send_sem=send, recv_sem=recv, device_id=device, device_id_type=MESH
        )

    def half_block(j, k, h):
        return phi.at[j, k, pl.ds(4 * h, 4)]

    def block_copy(j, route, src, dst, h, device):
        return remote(
            half_block(j, src, h), half_block(j, dst, h), phi_send.at[route, h, j], phi_recv.at[route, h, j], device
        )

    def own_sends(j):
        order = [(0, 0), (1, 1), (2, 0), (0, 1), (1, 0), (2, 1)]
        place = [(2 - way, partner), (2 - 2 * way, far), (2 + 2 * way, near)]
        return [block_copy(j, route, 2, place[route][0], h, place[route][1]) for route, h in order]

    def block_recv(j, route, h):
        place = [(2 + way, partner), (2 - 2 * way, near), (2 + 2 * way, far), (2 - way, partner)]
        return block_copy(j, route, 2, place[route][0], h, place[route][1])

    def forwards(j):
        return [
            block_copy(j, 3, 2 + way, 2 - way, 0, far),
            block_copy(j, 3, 2 + 2 * way, 2 + way, 1, partner),
        ]

    def keep(i, j, b):
        return screen[i, j * blocks + b].astype(F32)

    def tile(i, b):
        return slice(i * TILE, (i + 1) * TILE), slice(b * TILE, (b + 1) * TILE)

    piece = rows // (8 * CORES)
    tile_shape = (TILE // (CORES * piece), CORES, piece, TILE)

    def folded(i, b):
        wide = tile_shape[0]
        return slice(i * wide, (i + 1) * wide), slice(None), slice(None), slice(b * TILE, (b + 1) * TILE)

    def phi_tile(j, i, b):
        return phi[(j, 2, *folded(i, b))].reshape(TILE, TILE).astype(F32)

    def mask_own(j):
        for i in range(row_tiles):
            for b in range(blocks):
                r, c = tile(i, b)
                value = (raw0[j, r, c].astype(F32) * keep(i, j, b)).astype(BF16)
                phi[(j, 2, *folded(i, b))] = value.reshape(tile_shape)

    raw_copy(0).wait()
    mask_own(0)
    pl.semaphore_wait(barrier, len(peers))
    for copy in own_sends(0):
        copy.start()
    for j in range(1, steps):
        raw_copy(j).wait()
        mask_own(j)
        if j < DEPTH:
            for copy in own_sends(j):
                copy.start()

    dens_copy.wait()

    @pl.loop(0, rows // 32)
    def _(i):
        at = pl.multiple_of(i * 32, 32)
        whole = dens32[pl.ds(at, 32), :]
        high = whole.astype(BF16)
        dens_cat[pl.ds(at, 32), :] = high
        dens_cat[pl.ds(rows + at, 32), :] = (whole - high.astype(F32)).astype(BF16)

    acc[...] = jnp.zeros_like(acc)

    def a_copies(j):
        return [
            remote(part_a.at[j, 3], part_a.at[j, i], pa_send.at[j, i], pa_recv.at[j, i], peer)
            for i, peer in enumerate(group_a)
        ]

    def b_copies(j):
        return [
            remote(sum_a.at[j], part_b.at[j, i], pb_send.at[j, i], pb_recv.at[j, i], peer)
            for i, peer in enumerate(group_b)
        ]

    def density_step(j):
        applied[...] = jnp.dot(
            dens_cat[...], phi[j].reshape(BAND * rows, CHUNK), preferred_element_type=F32
        )
        for b in range(blocks):
            sums = [jnp.zeros((1, TILE), F32)] * 4
            for i in range(row_tiles):
                r, c = tile(i, b)
                low_rows = slice(rows + i * TILE, rows + (i + 1) * TILE)
                mine = (applied[r, c] + applied[low_rows, c]) * keep(i, j, b)
                sums[0] = sums[0] + jnp.sum(mine * phi_tile(j, i, b), axis=0, keepdims=True)
                for d in range(3):
                    sums[d + 1] = sums[d + 1] + jnp.sum(mine * comps[j, d, r, c].astype(F32), axis=0, keepdims=True)
            for d in range(4):
                part_a[j, 3, d * blocks + b : d * blocks + b + 1, :] = sums[d]

    def potential_step(j):
        total = sum_a[j]
        for i in range(3):
            total = total + part_b[j, i]
        point = total[0:blocks]
        grads = [2.0 * total[d * blocks : (d + 1) * blocks] for d in (1, 2, 3)]
        squared = grads[0] * grads[0] + grads[1] * grads[1] + grads[2] * grads[2]
        at = j * blocks
        lines = [quad[pl.ds(at + b, 1), :] * factor[atom[at + b]] for b in range(blocks)]
        weights = jnp.concatenate(lines, axis=0) * (1.0 / math.sqrt(points * 16))
        density_pot, gradient_pot = potentials(point, squared, core_dens[pl.ds(at, blocks), :])
        coef[0:blocks, :] = 0.5 * weights * density_pot
        for d in range(3):
            coef[(d + 1) * blocks : (d + 2) * blocks, :] = 2.0 * weights * gradient_pot * grads[d]
        for b in range(blocks):
            factors = [coef[d * blocks + b : d * blocks + b + 1, :] for d in range(4)]
            for i in range(row_tiles):
                r, c = tile(i, b)
                value = factors[0] * phi_tile(j, i, b)
                rest = factors[1] * comps[j, 0, r, c].astype(F32)
                for d in range(1, 3):
                    rest = rest + factors[d + 1] * comps[j, d, r, c].astype(F32)
                pot = ((value + rest) * keep(i, j, b)).astype(BF16)
                half[(j, *folded(i, b))] = pot.reshape(tile_shape)

    def sibling_blocks(j):
        ahead, other = pl.ds(2, 3), 1 - core
        return [
            remote(phi.at[j, ahead], phi_sib.at[j, ahead], c_send.at[0, j], c_recv.at[0, j], sibling),
            remote(
                phi.at[j, pl.ds(0, 2), :, other], phi_sib.at[j, pl.ds(0, 2), :, other],
                c_send.at[1, j], c_recv.at[1, j], sibling,
            ),
        ]

    def sibling_half(j):
        return remote(half.at[j], half_sib.at[j], c_send.at[2, j], c_recv.at[2, j], sibling)

    def matrix_part(j, block, pot, offsets):
        def contract(left, right):
            return lax.dot_general(left, right, (((1,), (1,)), ((), ())), preferred_element_type=F32)

        own_pot = pot[j, :, core].reshape(rows // CORES, CHUNK)
        all_pot = pot[j].reshape(rows, CHUNK)
        for k in offsets:
            term = 0.0
            if k <= 2:
                term = contract(block[j, k, :, core].reshape(rows // CORES, CHUNK), all_pot)
            if k >= 2:
                term = term + contract(own_pot, block[j, k].reshape(rows, CHUNK))
            acc[k] += term.reshape(acc.shape[1:])

    def pass_on(j):
        first, second = forwards(j)
        block_recv(j, 0, 0).wait_recv()
        first.start()
        block_recv(j, 2, 1).wait_recv()
        second.start()

    for j in range(LEAD):
        pass_on(j)

    @pl.loop(0, steps + LAG_B)
    def _(t):
        @pl.when(t + DEPTH < steps)
        def _():
            for copy in own_sends(t + DEPTH):
                copy.start()

        @pl.when(t + LEAD < steps)
        def _():
            pass_on(t + LEAD)

        @pl.when(t < steps)
        def _():
            for route, h in ((0, 1), (2, 0), (1, 0), (1, 1), (3, 0), (3, 1)):
                block_recv(t, route, h).wait_recv()
            for copy in sibling_blocks(t):
                copy.start()
            comp_copy(t).wait()
            density_step(t)
            for copy in a_copies(t):
                copy.start()

        @pl.when((t >= LAG_A) & (t < steps + LAG_A))
        def _():
            j = t - LAG_A
            for copy in a_copies(j):
                copy.wait_recv()
            sum_a[j] = (part_a[j, 3] + part_a[j, 0]) + (part_a[j, 1] + part_a[j, 2])
            for copy in b_copies(j):
                copy.start()

        @pl.when(t >= LAG_B)
        def _():
            j = t - LAG_B
            for copy in b_copies(j):
                copy.wait_recv()
            potential_step(j)
            sibling_half(j).start()
            matrix_part(j, phi, half, range(BAND))

        @pl.when(t >= LAG_B + 1)
        def _():
            j = t - LAG_B - 1
            for copy in (*sibling_blocks(j), sibling_half(j)):
                copy.wait_recv()
            matrix_part(j, phi_sib, half_sib, range(BAND))

    def first_copies(k):
        if k in X_FIRST:
            return [
                remote(
                    send.at[k, :, (chip_x + dx + 1) % X_CHIPS], recv_x.at[k, dx], r_send.at[k, dx], r_recv.at[k, dx], peer
                )
                for dx, peer in enumerate(along_x)
            ]
        return [remote(send.at[k, 1 - low], recv_y.at[k], r_send.at[k, 0], r_recv.at[k, 0], across_y)]

    def second_copies(k):
        if k == 0:
            return [
                remote(mid_y.at[k], got_y.at[k], m_send.at[k, 0], m_recv.at[k, 0], at_chip(1, 0, -2)),
                remote(fin, fin_recv, m_send.at[k, 1], m_recv.at[k, 1], at_chip(0, 0, -2)),
            ]
        if k == 1:
            return [
                remote(
                    mid_x.at[k, (chip_x + dx) % X_CHIPS], got_x1.at[dx], m_send.at[k, dx], m_recv.at[k, dx],
                    at_chip(0, dx, -1),
                )
                for dx in range(X_CHIPS)
            ]
        if k in X_FIRST:
            src, dst = (mid_y32, got_y32) if k == 2 else (mid_y.at[k], got_y.at[k])
            return [remote(src, dst, m_send.at[k, 0], m_recv.at[k, 0], across_y)]
        return [
            remote(
                mid_x.at[k, (chip_x + dx + 1) % X_CHIPS], got_x.at[k, dx], m_send.at[k, dx], m_recv.at[k, dx], peer
            )
            for dx, peer in enumerate(along_x)
        ]

    for copy in (*sibling_blocks(steps - 1), sibling_half(steps - 1)):
        copy.wait_recv()
    for k in range(BAND):
        matrix_part(steps - 1, phi_sib, half_sib, (k,))
        send[k] = acc[k].astype(BF16)
        for copy in first_copies(k):
            copy.start()

    for k in range(BAND):
        for copy in first_copies(k):
            copy.wait_recv()
        if k in X_FIRST:
            away = acc[k, 1 - low, chip_x]
            total = acc[k, low, chip_x]
            for dx in range(3):
                away = away + recv_x[k, dx, 1 - low].astype(F32)
                total = total + recv_x[k, dx, low].astype(F32)
            if k == 2:
                mid_y32[...] = away
            else:
                mid_y[k] = away.astype(BF16)
            if k == 0:
                fin[...] = total
            else:
                own[k] = total
        else:
            acc[k, low] = acc[k, low] + recv_y[k].astype(F32)
            mid_x[k] = acc[k, low].astype(BF16)
            if k > 1:
                own[k] = acc[k, low, chip_x]
        for copy in second_copies(k):
            copy.start()

    def collect(k):
        for copy in second_copies(k):
            copy.wait_recv()
        if k == 0:
            return fin_recv[...] + got_y[k].astype(F32)
        if k == 1:
            pieces = [got_x1[dx].astype(F32) for dx in range(X_CHIPS)]
            return (pieces[0] + pieces[1]) + (pieces[2] + pieces[3])
        total = own[k]
        if k == 2:
            return total + got_y32[...]
        if k in X_FIRST:
            return total + got_y[k].astype(F32)
        for dx in range(3):
            total = total + got_x[k, dx].astype(F32)
        return total

    out[:, 0:rows] = collect(2)
    for k in (1, 2):
        ahead = collect(2 - k)
        out[:, k * rows : (k + 1) * rows] = ahead + collect(k + 2)

    for j in range(steps):
        for copy in (*own_sends(j), *forwards(j)):
            copy.wait_send()
        for copy in (*a_copies(j), *b_copies(j), *sibling_blocks(j), sibling_half(j)):
            copy.wait_send()
    for k in range(BAND):
        for copy in first_copies(k) + second_copies(k):
            copy.wait_send()


def body(basis_values, density, screen, atom_of_block, atom_factor, quad_weight, core_density):
    rows, points = basis_values.shape[1:]
    steps = points // CHUNK
    piece = rows // 16
    dma = pltpu.SemaphoreType.DMA
    vmem, smem, hbm = (pl.BlockSpec(memory_space=s) for s in (pltpu.VMEM, pltpu.SMEM, pl.ANY))
    flat = 4 * CHUNK // TILE
    return pl.pallas_call(
        kernel,
        out_shape=jax.ShapeDtypeStruct((piece, 3 * rows), F32),
        in_specs=[hbm, hbm, smem, smem, smem, vmem, vmem],
        out_specs=vmem,
        scratch_shapes=[
            pltpu.VMEM((steps, rows, CHUNK), BF16),
            pltpu.VMEM((steps, 3, rows, CHUNK), BF16),
            pltpu.VMEM((rows, BAND * rows), F32),
            pltpu.VMEM((2 * rows, BAND * rows), BF16),
            pltpu.VMEM((steps, BAND, 8, CORES, piece, CHUNK), BF16),
            pltpu.VMEM((steps, BAND, 8, CORES, piece, CHUNK), BF16),
            pltpu.VMEM((2 * rows, CHUNK), F32),
            pltpu.VMEM((steps, 8, CORES, piece, CHUNK), BF16),
            pltpu.VMEM((steps, 8, CORES, piece, CHUNK), BF16),
            pltpu.VMEM((BAND, Y_LOW, X_CHIPS, piece, rows), F32),
            pltpu.VMEM((steps, 4, flat, TILE), F32),
            pltpu.VMEM((steps, 3, flat, TILE), F32),
            pltpu.VMEM((steps, flat, TILE), F32),
            pltpu.VMEM((flat, TILE), F32),
            pltpu.VMEM((BAND, Y_LOW, X_CHIPS, piece, rows), BF16),
            pltpu.VMEM((BAND, X_CHIPS - 1, Y_LOW, piece, rows), BF16),
            pltpu.VMEM((BAND, X_CHIPS, piece, rows), BF16),
            pltpu.VMEM((BAND, piece, rows), BF16),
            pltpu.VMEM((piece, rows), F32),
            pltpu.VMEM((BAND, X_CHIPS, piece, rows), BF16),
            pltpu.VMEM((BAND, piece, rows), BF16),
            pltpu.VMEM((piece, rows), F32),
            pltpu.VMEM((BAND, X_CHIPS - 1, piece, rows), BF16),
            pltpu.VMEM((X_CHIPS, piece, rows), BF16),
            pltpu.VMEM((BAND, piece, rows), F32),
            pltpu.VMEM((piece, rows), F32),
            pltpu.VMEM((piece, rows), F32),
            dma((steps,)), dma((steps,)), dma,
            dma((4, 2, steps)), dma((4, 2, steps)),
            dma((steps, 3)), dma((steps, 3)), dma((steps, 3)), dma((steps, 3)),
            dma((3, steps)), dma((3, steps)),
            dma((BAND, 3)), dma((BAND, 3)), dma((BAND, 4)), dma((BAND, 4)),
        ],
        compiler_params=pltpu.CompilerParams(
            collective_id=0, has_side_effects=True, vmem_limit_bytes=56 << 20
        ),
        name="xc_matrix",
    )(
        basis_values, density, screen, atom_of_block, atom_factor,
        quad_weight.reshape(-1, TILE), core_density.reshape(-1, TILE),
    )


def solution(mesh):
    in_specs = (
        P(None, "row", "col"),
        P("row", None),
        P("row", "col"),
        P("col"),
        P(),
        P("col"),
        P("col"),
    )
    out_specs = P(("row", "col"), None)
    return jax.shard_map(body, mesh=mesh, in_specs=in_specs, out_specs=out_specs, check_vma=False)
```

```python
import functools
import math

import jax
import jax.numpy as jnp
from jax import lax
from jax.experimental import pallas as pl
from jax.experimental.pallas import tpu as pltpu
from jax.sharding import PartitionSpec as P

F32, BF16 = jnp.float32, jnp.bfloat16
MESH = pl.DeviceIdType.MESH
BAND = 5
KAPPA_VALUE = 0.804
MU_VALUE = 0.22
SLATER_COEF = 0.7386

TILE = 128
CHUNK = 256
X_FIRST = (0, 2, 4)
X_CHIPS, Y_LOW, CORES, PLANES = 4, 2, 2, 8
DEPTH = 3
LEAD = 1
LAG_A, LAG_B = 1, 2


def potentials(point, squared, core):
    t_square = point * point + core * core
    log_t = 0.5 * jnp.log(t_square)
    reduced = squared * jnp.exp((-8.0 / 3.0) * log_t)
    inverse = 1.0 / (1.0 + (MU_VALUE / KAPPA_VALUE) * reduced)
    enhance = 1.0 + KAPPA_VALUE - KAPPA_VALUE * inverse
    slope = MU_VALUE * inverse * inverse
    slope_reduced = MU_VALUE * (reduced * inverse) * inverse
    along_t = -SLATER_COEF * jnp.exp((1.0 / 3.0) * log_t) * ((4.0 / 3.0) * enhance - (8.0 / 3.0) * slope_reduced)
    density_pot = along_t * (point * jnp.exp(-log_t))
    gradient_pot = -SLATER_COEF * slope * jnp.exp((-4.0 / 3.0) * log_t)
    return density_pot, gradient_pot


def kernel(
    basis, dens, screen, atom, factor, quad, core_dens, out,
    raw0, comps, dens32, dens_cat, phi, phi_sib, applied, half, half_sib, acc, part_a, part_b, sum_a, coef,
    send, recv_x, recv_y, mid_y, mid_y32, mid_x, got_y, got_y32, got_x, got_x1, own, fin, fin_recv,
    raw_sem, comp_sem, dens_sem, phi_send, phi_recv, pa_send, pa_recv, pb_send, pb_recv,
    c_send, c_recv, r_send, r_recv, m_send, m_recv,
):
    rows = basis.shape[1]
    points = basis.shape[2]
    steps = points // CHUNK
    blocks = CHUNK // TILE
    row_tiles = rows // TILE
    row, col = lax.axis_index("row"), lax.axis_index("col")
    plane, side = row // 2, row % 2
    low, chip_x, core = col // (X_CHIPS * CORES), (col // CORES) % X_CHIPS, col % CORES
    way = 1 - 2 * side

    def at_row(new_plane, new_side):
        return {"row": lax.rem(new_plane + PLANES, PLANES) * 2 + new_side, "col": col}

    def at_chip(dy, dx, offset=0):
        return {"row": lax.rem(row + offset + 16, 16), "col": (((low + dy) % Y_LOW) * X_CHIPS + (chip_x + dx) % X_CHIPS) * CORES + core}

    paired = plane + 1 - 2 * (plane % 2)
    partner = at_row(plane, 1 - side)
    far, near = at_row(plane + way, side), at_row(plane - way, side)
    odd = at_row(plane - way, 1 - side)
    group_a = [partner, at_row(paired, side), at_row(paired, 1 - side)]
    group_b = [at_row(plane + 2, side), at_row(plane + 4, side), at_row(plane + 6, side)]
    sibling = {"row": row, "col": col + 1 - 2 * core}
    across_y = at_chip(1, 0)
    along_x = [at_chip(0, dx) for dx in range(1, X_CHIPS)]
    shifted = [at_chip(1, 0, offset) for offset in (-2, 2)]
    shifted += [at_chip(0, dx, offset) for offset in (-1, 1) for dx in range(1, X_CHIPS)]

    def raw_copy(j):
        return pltpu.make_async_copy(basis.at[0, :, pl.ds(j * CHUNK, CHUNK)], raw0.at[j], raw_sem.at[j])

    def comp_copy(j):
        return pltpu.make_async_copy(basis.at[pl.ds(1, 3), :, pl.ds(j * CHUNK, CHUNK)], comps.at[j], comp_sem.at[j])

    dens_copy = pltpu.make_async_copy(dens, dens32, dens_sem)
    for j in range(steps):
        raw_copy(j).start()
    dens_copy.start()
    for j in range(steps):
        comp_copy(j).start()

    barrier = pltpu.get_barrier_semaphore()
    peers = [partner, far, near, odd, group_a[2], *group_b, sibling, across_y, *along_x, *shifted]
    for peer in peers:
        pl.semaphore_signal(barrier, inc=1, device_id=peer, device_id_type=MESH)

    def remote(src, dst, send, recv, device):
        return pltpu.make_async_remote_copy(
            src_ref=src, dst_ref=dst, send_sem=send, recv_sem=recv, device_id=device, device_id_type=MESH
        )

    def half_block(j, k, h):
        return phi.at[j, k, pl.ds(4 * h, 4)]

    def block_copy(j, route, src, dst, h, device):
        return remote(
            half_block(j, src, h), half_block(j, dst, h), phi_send.at[route, h, j], phi_recv.at[route, h, j], device
        )

    def own_sends(j):
        order = [(0, 0), (2, 1), (0, 1), (1, 0), (1, 1), (2, 0)]
        place = [(2 - way, partner), (2 - 2 * way, far), (2 + 2 * way, near)]
        return [block_copy(j, route, 2, place[route][0], h, place[route][1]) for route, h in order]

    def block_recv(j, route, h):
        place = [(2 + way, partner), (2 - 2 * way, near), (2 + 2 * way, far), (2 - way, partner)]
        return block_copy(j, route, 2, place[route][0], h, place[route][1])

    def forwards(j):
        return [
            block_copy(j, 3, 2 + way, 2 - way, 0, far),
            block_copy(j, 3, 2 + 2 * way, 2 + way, 1, partner),
        ]

    def keep(i, j, b):
        return screen[i, j * blocks + b].astype(F32)

    def tile(i, b):
        return slice(i * TILE, (i + 1) * TILE), slice(b * TILE, (b + 1) * TILE)

    piece = rows // (8 * CORES)
    tile_shape = (TILE // (CORES * piece), CORES, piece, TILE)

    def folded(i, b):
        wide = tile_shape[0]
        return slice(i * wide, (i + 1) * wide), slice(None), slice(None), slice(b * TILE, (b + 1) * TILE)

    def phi_tile(j, i, b):
        return phi[(j, 2, *folded(i, b))].reshape(TILE, TILE).astype(F32)

    def mask_own(j):
        for i in range(row_tiles):
            for b in range(blocks):
                r, c = tile(i, b)
                value = (raw0[j, r, c].astype(F32) * keep(i, j, b)).astype(BF16)
                phi[(j, 2, *folded(i, b))] = value.reshape(tile_shape)

    raw_copy(0).wait()
    mask_own(0)
    pl.semaphore_wait(barrier, len(peers))
    for copy in own_sends(0):
        copy.start()
    for j in range(1, steps):
        raw_copy(j).wait()
        mask_own(j)
        if j < DEPTH:
            for copy in own_sends(j):
                copy.start()

    dens_copy.wait()

    @pl.loop(0, rows // 32)
    def _(i):
        at = pl.multiple_of(i * 32, 32)
        whole = dens32[pl.ds(at, 32), :]
        high = whole.astype(BF16)
        dens_cat[pl.ds(at, 32), :] = high
        dens_cat[pl.ds(rows + at, 32), :] = (whole - high.astype(F32)).astype(BF16)

    acc[...] = jnp.zeros_like(acc)

    def a_copies(j):
        return [
            remote(part_a.at[j, 3], part_a.at[j, i], pa_send.at[j, i], pa_recv.at[j, i], peer)
            for i, peer in enumerate(group_a)
        ]

    def b_copies(j):
        return [
            remote(sum_a.at[j], part_b.at[j, i], pb_send.at[j, i], pb_recv.at[j, i], peer)
            for i, peer in enumerate(group_b)
        ]

    def density_step(j):
        applied[...] = jnp.dot(
            dens_cat[...], phi[j].reshape(BAND * rows, CHUNK), preferred_element_type=F32
        )
        for b in range(blocks):
            sums = [jnp.zeros((1, TILE), F32)] * 4
            for i in range(row_tiles):
                r, c = tile(i, b)
                low_rows = slice(rows + i * TILE, rows + (i + 1) * TILE)
                mine = (applied[r, c] + applied[low_rows, c]) * keep(i, j, b)
                sums[0] = sums[0] + jnp.sum(mine * phi_tile(j, i, b), axis=0, keepdims=True)
                for d in range(3):
                    sums[d + 1] = sums[d + 1] + jnp.sum(mine * comps[j, d, r, c].astype(F32), axis=0, keepdims=True)
            for d in range(4):
                part_a[j, 3, d * blocks + b : d * blocks + b + 1, :] = sums[d]

    def potential_step(j):
        total = sum_a[j]
        for i in range(3):
            total = total + part_b[j, i]
        point = total[0:blocks]
        grads = [2.0 * total[d * blocks : (d + 1) * blocks] for d in (1, 2, 3)]
        squared = grads[0] * grads[0] + grads[1] * grads[1] + grads[2] * grads[2]
        at = j * blocks
        lines = [quad[pl.ds(at + b, 1), :] * factor[atom[at + b]] for b in range(blocks)]
        weights = jnp.concatenate(lines, axis=0) * (1.0 / math.sqrt(points * 16))
        density_pot, gradient_pot = potentials(point, squared, core_dens[pl.ds(at, blocks), :])
        coef[0:blocks, :] = 0.5 * weights * density_pot
        for d in range(3):
            coef[(d + 1) * blocks : (d + 2) * blocks, :] = 2.0 * weights * gradient_pot * grads[d]
        for b in range(blocks):
            factors = [coef[d * blocks + b : d * blocks + b + 1, :] for d in range(4)]
            for i in range(row_tiles):
                r, c = tile(i, b)
                value = factors[0] * phi_tile(j, i, b)
                rest = factors[1] * comps[j, 0, r, c].astype(F32)
                for d in range(1, 3):
                    rest = rest + factors[d + 1] * comps[j, d, r, c].astype(F32)
                pot = ((value + rest) * keep(i, j, b)).astype(BF16)
                half[(j, *folded(i, b))] = pot.reshape(tile_shape)

    def sibling_blocks(j):
        ahead, other = pl.ds(2, 3), 1 - core
        return [
            remote(phi.at[j, ahead], phi_sib.at[j, ahead], c_send.at[0, j], c_recv.at[0, j], sibling),
            remote(
                phi.at[j, pl.ds(0, 2), :, other], phi_sib.at[j, pl.ds(0, 2), :, other],
                c_send.at[1, j], c_recv.at[1, j], sibling,
            ),
        ]

    def sibling_half(j):
        return remote(half.at[j], half_sib.at[j], c_send.at[2, j], c_recv.at[2, j], sibling)

    def matrix_part(j, block, pot, offsets):
        def contract(left, right):
            return lax.dot_general(left, right, (((1,), (1,)), ((), ())), preferred_element_type=F32)

        own_pot = pot[j, :, core].reshape(rows // CORES, CHUNK)
        all_pot = pot[j].reshape(rows, CHUNK)
        for k in offsets:
            term = 0.0
            if k <= 2:
                term = contract(block[j, k, :, core].reshape(rows // CORES, CHUNK), all_pot)
            if k >= 2:
                term = term + contract(own_pot, block[j, k].reshape(rows, CHUNK))
            acc[k] += term.reshape(acc.shape[1:])

    def pass_on(j):
        first, second = forwards(j)
        block_recv(j, 0, 0).wait_recv()
        first.start()
        block_recv(j, 2, 1).wait_recv()
        second.start()

    for j in range(LEAD):
        pass_on(j)

    @pl.loop(0, steps + LAG_B)
    def _(t):
        @pl.when(t + DEPTH < steps)
        def _():
            for copy in own_sends(t + DEPTH):
                copy.start()

        @pl.when(t + LEAD < steps)
        def _():
            pass_on(t + LEAD)

        @pl.when(t < steps)
        def _():
            for route, h in ((0, 1), (2, 0), (1, 0), (1, 1), (3, 0), (3, 1)):
                block_recv(t, route, h).wait_recv()
            for copy in sibling_blocks(t):
                copy.start()
            comp_copy(t).wait()
            density_step(t)
            for copy in a_copies(t):
                copy.start()

        @pl.when((t >= LAG_A) & (t < steps + LAG_A))
        def _():
            j = t - LAG_A
            for copy in a_copies(j):
                copy.wait_recv()
            sum_a[j] = (part_a[j, 3] + part_a[j, 0]) + (part_a[j, 1] + part_a[j, 2])
            for copy in b_copies(j):
                copy.start()

        @pl.when(t >= LAG_B)
        def _():
            j = t - LAG_B
            for copy in b_copies(j):
                copy.wait_recv()
            potential_step(j)
            sibling_half(j).start()
            matrix_part(j, phi, half, range(BAND))

        @pl.when(t >= LAG_B + 1)
        def _():
            j = t - LAG_B - 1
            for copy in (*sibling_blocks(j), sibling_half(j)):
                copy.wait_recv()
            matrix_part(j, phi_sib, half_sib, range(BAND))

    def first_copies(k):
        if k in X_FIRST:
            return [
                remote(
                    send.at[k, :, (chip_x + dx + 1) % X_CHIPS], recv_x.at[k, dx], r_send.at[k, dx], r_recv.at[k, dx], peer
                )
                for dx, peer in enumerate(along_x)
            ]
        return [remote(send.at[k, 1 - low], recv_y.at[k], r_send.at[k, 0], r_recv.at[k, 0], across_y)]

    def second_copies(k):
        if k == 0:
            return [
                remote(mid_y.at[k], got_y.at[k], m_send.at[k, 0], m_recv.at[k, 0], at_chip(1, 0, -2)),
                remote(fin, fin_recv, m_send.at[k, 1], m_recv.at[k, 1], at_chip(0, 0, -2)),
            ]
        if k == 1:
            return [
                remote(
                    mid_x.at[k, (chip_x + dx) % X_CHIPS], got_x1.at[dx], m_send.at[k, dx], m_recv.at[k, dx],
                    at_chip(0, dx, -1),
                )
                for dx in range(X_CHIPS)
            ]
        if k in X_FIRST:
            src, dst = (mid_y32, got_y32) if k == 2 else (mid_y.at[k], got_y.at[k])
            return [remote(src, dst, m_send.at[k, 0], m_recv.at[k, 0], across_y)]
        return [
            remote(
                mid_x.at[k, (chip_x + dx + 1) % X_CHIPS], got_x.at[k, dx], m_send.at[k, dx], m_recv.at[k, dx], peer
            )
            for dx, peer in enumerate(along_x)
        ]

    for copy in (*sibling_blocks(steps - 1), sibling_half(steps - 1)):
        copy.wait_recv()
    for k in range(BAND):
        matrix_part(steps - 1, phi_sib, half_sib, (k,))
        send[k] = acc[k].astype(BF16)
        for copy in first_copies(k):
            copy.start()

    for j in range(steps):
        for copy in (*own_sends(j), *forwards(j)):
            copy.wait_send()
        for copy in (*a_copies(j), *b_copies(j), *sibling_blocks(j), sibling_half(j)):
            copy.wait_send()

    for k in range(BAND):
        for copy in first_copies(k):
            copy.wait_recv()
        if k in X_FIRST:
            away = acc[k, 1 - low, chip_x]
            total = acc[k, low, chip_x]
            for dx in range(3):
                away = away + recv_x[k, dx, 1 - low].astype(F32)
                total = total + recv_x[k, dx, low].astype(F32)
            if k == 2:
                mid_y32[...] = away
            else:
                mid_y[k] = away.astype(BF16)
            if k == 0:
                fin[...] = total
            else:
                own[k] = total
        else:
            acc[k, low] = acc[k, low] + recv_y[k].astype(F32)
            mid_x[k] = acc[k, low].astype(BF16)
            if k > 1:
                own[k] = acc[k, low, chip_x]
        for copy in second_copies(k):
            copy.start()

    def collect(k):
        for copy in second_copies(k):
            copy.wait_recv()
        if k == 0:
            return fin_recv[...] + got_y[k].astype(F32)
        if k == 1:
            pieces = [got_x1[dx].astype(F32) for dx in range(X_CHIPS)]
            return (pieces[0] + pieces[1]) + (pieces[2] + pieces[3])
        total = own[k]
        if k == 2:
            return total + got_y32[...]
        if k in X_FIRST:
            return total + got_y[k].astype(F32)
        for dx in range(3):
            total = total + got_x[k, dx].astype(F32)
        return total

    out[:, 0:rows] = collect(2)
    for k in (1, 2):
        ahead = collect(2 - k)
        out[:, k * rows : (k + 1) * rows] = ahead + collect(k + 2)

    for k in range(BAND):
        for copy in first_copies(k) + second_copies(k):
            copy.wait_send()


def body(basis_values, density, screen, atom_of_block, atom_factor, quad_weight, core_density):
    rows, points = basis_values.shape[1:]
    steps = points // CHUNK
    piece = rows // 16
    dma = pltpu.SemaphoreType.DMA
    vmem, smem, hbm = (pl.BlockSpec(memory_space=s) for s in (pltpu.VMEM, pltpu.SMEM, pl.ANY))
    flat = 4 * CHUNK // TILE
    return pl.pallas_call(
        kernel,
        out_shape=jax.ShapeDtypeStruct((piece, 3 * rows), F32),
        in_specs=[hbm, hbm, smem, smem, smem, vmem, vmem],
        out_specs=vmem,
        scratch_shapes=[
            pltpu.VMEM((steps, rows, CHUNK), BF16),
            pltpu.VMEM((steps, 3, rows, CHUNK), BF16),
            pltpu.VMEM((rows, BAND * rows), F32),
            pltpu.VMEM((2 * rows, BAND * rows), BF16),
            pltpu.VMEM((steps, BAND, 8, CORES, piece, CHUNK), BF16),
            pltpu.VMEM((steps, BAND, 8, CORES, piece, CHUNK), BF16),
            pltpu.VMEM((2 * rows, CHUNK), F32),
            pltpu.VMEM((steps, 8, CORES, piece, CHUNK), BF16),
            pltpu.VMEM((steps, 8, CORES, piece, CHUNK), BF16),
            pltpu.VMEM((BAND, Y_LOW, X_CHIPS, piece, rows), F32),
            pltpu.VMEM((steps, 4, flat, TILE), F32),
            pltpu.VMEM((steps, 3, flat, TILE), F32),
            pltpu.VMEM((steps, flat, TILE), F32),
            pltpu.VMEM((flat, TILE), F32),
            pltpu.VMEM((BAND, Y_LOW, X_CHIPS, piece, rows), BF16),
            pltpu.VMEM((BAND, X_CHIPS - 1, Y_LOW, piece, rows), BF16),
            pltpu.VMEM((BAND, X_CHIPS, piece, rows), BF16),
            pltpu.VMEM((BAND, piece, rows), BF16),
            pltpu.VMEM((piece, rows), F32),
            pltpu.VMEM((BAND, X_CHIPS, piece, rows), BF16),
            pltpu.VMEM((BAND, piece, rows), BF16),
            pltpu.VMEM((piece, rows), F32),
            pltpu.VMEM((BAND, X_CHIPS - 1, piece, rows), BF16),
            pltpu.VMEM((X_CHIPS, piece, rows), BF16),
            pltpu.VMEM((BAND, piece, rows), F32),
            pltpu.VMEM((piece, rows), F32),
            pltpu.VMEM((piece, rows), F32),
            dma((steps,)), dma((steps,)), dma,
            dma((4, 2, steps)), dma((4, 2, steps)),
            dma((steps, 3)), dma((steps, 3)), dma((steps, 3)), dma((steps, 3)),
            dma((3, steps)), dma((3, steps)),
            dma((BAND, 3)), dma((BAND, 3)), dma((BAND, 4)), dma((BAND, 4)),
        ],
        compiler_params=pltpu.CompilerParams(
            collective_id=0, has_side_effects=True, vmem_limit_bytes=56 << 20
        ),
        name="xc_matrix",
    )(
        basis_values, density, screen, atom_of_block, atom_factor,
        quad_weight.reshape(-1, TILE), core_density.reshape(-1, TILE),
    )


def solution(mesh):
    in_specs = (
        P(None, "row", "col"),
        P("row", None),
        P("row", "col"),
        P("col"),
        P(),
        P("col"),
        P("col"),
    )
    out_specs = P(("row", "col"), None)
    return jax.shard_map(body, mesh=mesh, in_specs=in_specs, out_specs=out_specs, check_vma=False)
```

```python
import functools
import math

import jax
import jax.numpy as jnp
from jax import lax
from jax.experimental import pallas as pl
from jax.experimental.pallas import tpu as pltpu
from jax.sharding import PartitionSpec as P

F32, BF16 = jnp.float32, jnp.bfloat16
MESH = pl.DeviceIdType.MESH
BAND = 5
KAPPA_VALUE = 0.804
MU_VALUE = 0.22
SLATER_COEF = 0.7386

TILE = 128
CHUNK = 256
X_FIRST = (0, 2, 4)
X_CHIPS, Y_LOW, CORES, PLANES = 4, 2, 2, 8
DEPTH = 3
LEAD = 1
LAG_A, LAG_B = 1, 2


def potentials(point, squared, core):
    t_square = point * point + core * core
    log_t = 0.5 * jnp.log(t_square)
    reduced = squared * jnp.exp((-8.0 / 3.0) * log_t)
    inverse = 1.0 / (1.0 + (MU_VALUE / KAPPA_VALUE) * reduced)
    enhance = 1.0 + KAPPA_VALUE - KAPPA_VALUE * inverse
    slope = MU_VALUE * inverse * inverse
    slope_reduced = MU_VALUE * (reduced * inverse) * inverse
    along_t = -SLATER_COEF * jnp.exp((1.0 / 3.0) * log_t) * ((4.0 / 3.0) * enhance - (8.0 / 3.0) * slope_reduced)
    density_pot = along_t * (point * jnp.exp(-log_t))
    gradient_pot = -SLATER_COEF * slope * jnp.exp((-4.0 / 3.0) * log_t)
    return density_pot, gradient_pot


def kernel(
    basis, dens, screen, atom, factor, quad, core_dens, out,
    raw0, comps, dens32, dens_cat, phi, phi_sib, applied, half, half_sib, acc, part_a, part_b, sum_a, coef,
    send, recv_x, recv_y, mid_y, mid_y32, mid_x, got_y, got_y32, got_x, got_x1, own, fin, fin_recv,
    raw_sem, comp_sem, dens_sem, phi_send, phi_recv, pa_send, pa_recv, pb_send, pb_recv,
    c_send, c_recv, r_send, r_recv, m_send, m_recv,
):
    rows = basis.shape[1]
    points = basis.shape[2]
    steps = points // CHUNK
    blocks = CHUNK // TILE
    row_tiles = rows // TILE
    row, col = lax.axis_index("row"), lax.axis_index("col")
    plane, side = row // 2, row % 2
    low, chip_x, core = col // (X_CHIPS * CORES), (col // CORES) % X_CHIPS, col % CORES
    way = 1 - 2 * side

    def at_row(new_plane, new_side):
        return {"row": lax.rem(new_plane + PLANES, PLANES) * 2 + new_side, "col": col}

    def at_chip(dy, dx, offset=0):
        return {"row": lax.rem(row + offset + 16, 16), "col": (((low + dy) % Y_LOW) * X_CHIPS + (chip_x + dx) % X_CHIPS) * CORES + core}

    paired = plane + 1 - 2 * (plane % 2)
    partner = at_row(plane, 1 - side)
    far, near = at_row(plane + way, side), at_row(plane - way, side)
    odd = at_row(plane - way, 1 - side)
    group_a = [partner, at_row(paired, side), at_row(paired, 1 - side)]
    group_b = [at_row(plane + 2, side), at_row(plane + 4, side), at_row(plane + 6, side)]
    sibling = {"row": row, "col": col + 1 - 2 * core}
    across_y = at_chip(1, 0)
    along_x = [at_chip(0, dx) for dx in range(1, X_CHIPS)]
    shifted = [at_chip(1, 0, offset) for offset in (-2, 2)]
    shifted += [at_chip(0, dx, offset) for offset in (-1, 1) for dx in range(1, X_CHIPS)]

    def raw_copy(j):
        return pltpu.make_async_copy(basis.at[0, :, pl.ds(j * CHUNK, CHUNK)], raw0.at[j], raw_sem.at[j])

    def comp_copy(j):
        return pltpu.make_async_copy(basis.at[pl.ds(1, 3), :, pl.ds(j * CHUNK, CHUNK)], comps.at[j], comp_sem.at[j])

    dens_copy = pltpu.make_async_copy(dens, dens32, dens_sem)
    for j in range(steps):
        raw_copy(j).start()
    dens_copy.start()
    for j in range(steps):
        comp_copy(j).start()

    barrier = pltpu.get_barrier_semaphore()
    peers = [partner, far, near, odd, group_a[2], *group_b, sibling, across_y, *along_x, *shifted]
    for peer in peers:
        pl.semaphore_signal(barrier, inc=1, device_id=peer, device_id_type=MESH)

    def remote(src, dst, send, recv, device):
        return pltpu.make_async_remote_copy(
            src_ref=src, dst_ref=dst, send_sem=send, recv_sem=recv, device_id=device, device_id_type=MESH
        )

    def half_block(j, k, h):
        return phi.at[j, k, pl.ds(4 * h, 4)]

    def block_copy(j, route, src, dst, h, device):
        return remote(
            half_block(j, src, h), half_block(j, dst, h), phi_send.at[route, h, j], phi_recv.at[route, h, j], device
        )

    def own_sends(j):
        order = [(0, 0), (1, 1), (2, 0), (0, 1), (1, 0), (2, 1)]
        place = [(2 - way, partner), (2 - 2 * way, far), (2 + 2 * way, near)]
        return [block_copy(j, route, 2, place[route][0], h, place[route][1]) for route, h in order]

    def block_recv(j, route, h):
        place = [(2 + way, partner), (2 - 2 * way, near), (2 + 2 * way, far), (2 - way, partner)]
        return block_copy(j, route, 2, place[route][0], h, place[route][1])

    def forwards(j):
        return [
            block_copy(j, 3, 2 + way, 2 - way, 0, far),
            block_copy(j, 3, 2 + 2 * way, 2 + way, 1, partner),
        ]

    def keep(i, j, b):
        return screen[i, j * blocks + b].astype(F32)

    def tile(i, b):
        return slice(i * TILE, (i + 1) * TILE), slice(b * TILE, (b + 1) * TILE)

    piece = rows // (8 * CORES)
    tile_shape = (TILE // (CORES * piece), CORES, piece, TILE)

    def folded(i, b):
        wide = tile_shape[0]
        return slice(i * wide, (i + 1) * wide), slice(None), slice(None), slice(b * TILE, (b + 1) * TILE)

    def phi_tile(j, i, b):
        return phi[(j, 2, *folded(i, b))].reshape(TILE, TILE).astype(F32)

    def mask_own(j):
        for i in range(row_tiles):
            for b in range(blocks):
                r, c = tile(i, b)
                value = (raw0[j, r, c].astype(F32) * keep(i, j, b)).astype(BF16)
                phi[(j, 2, *folded(i, b))] = value.reshape(tile_shape)

    raw_copy(0).wait()
    mask_own(0)
    pl.semaphore_wait(barrier, len(peers))
    for copy in own_sends(0):
        copy.start()
    for j in range(1, steps):
        raw_copy(j).wait()
        mask_own(j)
        if j < DEPTH:
            for copy in own_sends(j):
                copy.start()

    dens_copy.wait()

    @pl.loop(0, rows // 32)
    def _(i):
        at = pl.multiple_of(i * 32, 32)
        whole = dens32[pl.ds(at, 32), :]
        high = whole.astype(BF16)
        dens_cat[pl.ds(at, 32), :] = high
        dens_cat[pl.ds(rows + at, 32), :] = (whole - high.astype(F32)).astype(BF16)

    acc[...] = jnp.zeros_like(acc)

    def a_copies(j):
        return [
            remote(part_a.at[j, 3], part_a.at[j, i], pa_send.at[j, i], pa_recv.at[j, i], peer)
            for i, peer in enumerate(group_a)
        ]

    def b_copies(j):
        return [
            remote(sum_a.at[j], part_b.at[j, i], pb_send.at[j, i], pb_recv.at[j, i], peer)
            for i, peer in enumerate(group_b)
        ]

    def density_step(j):
        applied[...] = jnp.dot(
            dens_cat[...], phi[j].reshape(BAND * rows, CHUNK), preferred_element_type=F32
        )
        for b in range(blocks):
            sums = [jnp.zeros((1, TILE), F32)] * 4
            for i in range(row_tiles):
                r, c = tile(i, b)
                low_rows = slice(rows + i * TILE, rows + (i + 1) * TILE)
                mine = (applied[r, c] + applied[low_rows, c]) * keep(i, j, b)
                sums[0] = sums[0] + jnp.sum(mine * phi_tile(j, i, b), axis=0, keepdims=True)
                for d in range(3):
                    sums[d + 1] = sums[d + 1] + jnp.sum(mine * comps[j, d, r, c].astype(F32), axis=0, keepdims=True)
            for d in range(4):
                part_a[j, 3, d * blocks + b : d * blocks + b + 1, :] = sums[d]

    def potential_step(j):
        total = sum_a[j]
        for i in range(3):
            total = total + part_b[j, i]
        point = total[0:blocks]
        grads = [2.0 * total[d * blocks : (d + 1) * blocks] for d in (1, 2, 3)]
        squared = grads[0] * grads[0] + grads[1] * grads[1] + grads[2] * grads[2]
        at = j * blocks
        lines = [quad[pl.ds(at + b, 1), :] * factor[atom[at + b]] for b in range(blocks)]
        weights = jnp.concatenate(lines, axis=0) * (1.0 / math.sqrt(points * 16))
        density_pot, gradient_pot = potentials(point, squared, core_dens[pl.ds(at, blocks), :])
        coef[0:blocks, :] = 0.5 * weights * density_pot
        for d in range(3):
            coef[(d + 1) * blocks : (d + 2) * blocks, :] = 2.0 * weights * gradient_pot * grads[d]
        for b in range(blocks):
            factors = [coef[d * blocks + b : d * blocks + b + 1, :] for d in range(4)]
            for i in range(row_tiles):
                r, c = tile(i, b)
                value = factors[0] * phi_tile(j, i, b)
                rest = factors[1] * comps[j, 0, r, c].astype(F32)
                for d in range(1, 3):
                    rest = rest + factors[d + 1] * comps[j, d, r, c].astype(F32)
                pot = ((value + rest) * keep(i, j, b)).astype(BF16)
                half[(j, *folded(i, b))] = pot.reshape(tile_shape)

    def sibling_blocks(j):
        ahead, other = pl.ds(2, 3), 1 - core
        return [
            remote(phi.at[j, ahead], phi_sib.at[j, ahead], c_send.at[0, j], c_recv.at[0, j], sibling),
            remote(
                phi.at[j, pl.ds(0, 2), :, other], phi_sib.at[j, pl.ds(0, 2), :, other],
                c_send.at[1, j], c_recv.at[1, j], sibling,
            ),
        ]

    def sibling_half(j):
        return remote(half.at[j], half_sib.at[j], c_send.at[2, j], c_recv.at[2, j], sibling)

    def matrix_part(j, block, pot, offsets):
        def contract(left, right):
            return lax.dot_general(left, right, (((1,), (1,)), ((), ())), preferred_element_type=F32)

        own_pot = pot[j, :, core].reshape(rows // CORES, CHUNK)
        all_pot = pot[j].reshape(rows, CHUNK)
        for k in offsets:
            term = 0.0
            if k <= 2:
                term = contract(block[j, k, :, core].reshape(rows // CORES, CHUNK), all_pot)
            if k >= 2:
                term = term + contract(own_pot, block[j, k].reshape(rows, CHUNK))
            acc[k] += term.reshape(acc.shape[1:])

    def pass_on(j):
        first, second = forwards(j)
        block_recv(j, 0, 0).wait_recv()
        first.start()
        block_recv(j, 2, 1).wait_recv()
        second.start()

    for j in range(LEAD):
        pass_on(j)

    @pl.loop(0, steps + LAG_B)
    def _(t):
        @pl.when(t + DEPTH < steps)
        def _():
            for copy in own_sends(t + DEPTH):
                copy.start()

        @pl.when(t + LEAD < steps)
        def _():
            pass_on(t + LEAD)

        @pl.when(t < steps)
        def _():
            for route, h in ((0, 1), (2, 0), (1, 0), (1, 1), (3, 0), (3, 1)):
                block_recv(t, route, h).wait_recv()
            for copy in sibling_blocks(t):
                copy.start()
            comp_copy(t).wait()
            density_step(t)
            for copy in a_copies(t):
                copy.start()

        @pl.when((t >= LAG_A) & (t < steps + LAG_A))
        def _():
            j = t - LAG_A
            for copy in a_copies(j):
                copy.wait_recv()
            sum_a[j] = (part_a[j, 3] + part_a[j, 0]) + (part_a[j, 1] + part_a[j, 2])
            for copy in b_copies(j):
                copy.start()

        @pl.when(t >= LAG_B)
        def _():
            j = t - LAG_B
            for copy in b_copies(j):
                copy.wait_recv()
            potential_step(j)
            sibling_half(j).start()
            matrix_part(j, phi, half, range(BAND))

        @pl.when(t >= LAG_B + 1)
        def _():
            j = t - LAG_B - 1
            for copy in (*sibling_blocks(j), sibling_half(j)):
                copy.wait_recv()
            matrix_part(j, phi_sib, half_sib, range(BAND))

    def first_copies(k):
        if k in X_FIRST:
            return [
                remote(
                    send.at[k, :, (chip_x + dx + 1) % X_CHIPS], recv_x.at[k, dx], r_send.at[k, dx], r_recv.at[k, dx], peer
                )
                for dx, peer in enumerate(along_x)
            ]
        return [remote(send.at[k, 1 - low], recv_y.at[k], r_send.at[k, 0], r_recv.at[k, 0], across_y)]

    def second_copies(k):
        if k == 0:
            return [
                remote(mid_y.at[k], got_y.at[k], m_send.at[k, 0], m_recv.at[k, 0], at_chip(1, 0, -2)),
                remote(fin, fin_recv, m_send.at[k, 1], m_recv.at[k, 1], at_chip(0, 0, -2)),
            ]
        if k == 1:
            return [
                remote(
                    mid_x.at[k, (chip_x + dx) % X_CHIPS], got_x1.at[dx], m_send.at[k, dx], m_recv.at[k, dx],
                    at_chip(0, dx, -1),
                )
                for dx in range(X_CHIPS)
            ]
        if k in X_FIRST:
            src, dst = (mid_y32, got_y32) if k == 2 else (mid_y.at[k], got_y.at[k])
            return [remote(src, dst, m_send.at[k, 0], m_recv.at[k, 0], across_y)]
        return [
            remote(
                mid_x.at[k, (chip_x + dx + 1) % X_CHIPS], got_x.at[k, dx], m_send.at[k, dx], m_recv.at[k, dx], peer
            )
            for dx, peer in enumerate(along_x)
        ]

    for copy in (*sibling_blocks(steps - 1), sibling_half(steps - 1)):
        copy.wait_recv()
    for k in (2, 1, 0, 3, 4):
        matrix_part(steps - 1, phi_sib, half_sib, (k,))
        send[k] = acc[k].astype(BF16)
        for copy in first_copies(k):
            copy.start()

    for k in (2, 1, 0, 3, 4):
        for copy in first_copies(k):
            copy.wait_recv()
        if k in X_FIRST:
            away = acc[k, 1 - low, chip_x]
            total = acc[k, low, chip_x]
            for dx in range(3):
                away = away + recv_x[k, dx, 1 - low].astype(F32)
                total = total + recv_x[k, dx, low].astype(F32)
            if k == 2:
                mid_y32[...] = away
            else:
                mid_y[k] = away.astype(BF16)
            if k == 0:
                fin[...] = total
            else:
                own[k] = total
        else:
            acc[k, low] = acc[k, low] + recv_y[k].astype(F32)
            mid_x[k] = acc[k, low].astype(BF16)
            if k > 1:
                own[k] = acc[k, low, chip_x]
        for copy in second_copies(k):
            copy.start()

    def collect(k):
        for copy in second_copies(k):
            copy.wait_recv()
        if k == 0:
            return fin_recv[...] + got_y[k].astype(F32)
        if k == 1:
            pieces = [got_x1[dx].astype(F32) for dx in range(X_CHIPS)]
            return (pieces[0] + pieces[1]) + (pieces[2] + pieces[3])
        total = own[k]
        if k == 2:
            return total + got_y32[...]
        if k in X_FIRST:
            return total + got_y[k].astype(F32)
        for dx in range(3):
            total = total + got_x[k, dx].astype(F32)
        return total

    out[:, 0:rows] = collect(2)
    for k in (1, 2):
        ahead = collect(2 - k)
        out[:, k * rows : (k + 1) * rows] = ahead + collect(k + 2)

    for j in range(steps):
        for copy in (*own_sends(j), *forwards(j)):
            copy.wait_send()
        for copy in (*a_copies(j), *b_copies(j), *sibling_blocks(j), sibling_half(j)):
            copy.wait_send()
    for k in range(BAND):
        for copy in first_copies(k) + second_copies(k):
            copy.wait_send()


def body(basis_values, density, screen, atom_of_block, atom_factor, quad_weight, core_density):
    rows, points = basis_values.shape[1:]
    steps = points // CHUNK
    piece = rows // 16
    dma = pltpu.SemaphoreType.DMA
    vmem, smem, hbm = (pl.BlockSpec(memory_space=s) for s in (pltpu.VMEM, pltpu.SMEM, pl.ANY))
    flat = 4 * CHUNK // TILE
    return pl.pallas_call(
        kernel,
        out_shape=jax.ShapeDtypeStruct((piece, 3 * rows), F32),
        in_specs=[hbm, hbm, smem, smem, smem, vmem, vmem],
        out_specs=vmem,
        scratch_shapes=[
            pltpu.VMEM((steps, rows, CHUNK), BF16),
            pltpu.VMEM((steps, 3, rows, CHUNK), BF16),
            pltpu.VMEM((rows, BAND * rows), F32),
            pltpu.VMEM((2 * rows, BAND * rows), BF16),
            pltpu.VMEM((steps, BAND, 8, CORES, piece, CHUNK), BF16),
            pltpu.VMEM((steps, BAND, 8, CORES, piece, CHUNK), BF16),
            pltpu.VMEM((2 * rows, CHUNK), F32),
            pltpu.VMEM((steps, 8, CORES, piece, CHUNK), BF16),
            pltpu.VMEM((steps, 8, CORES, piece, CHUNK), BF16),
            pltpu.VMEM((BAND, Y_LOW, X_CHIPS, piece, rows), F32),
            pltpu.VMEM((steps, 4, flat, TILE), F32),
            pltpu.VMEM((steps, 3, flat, TILE), F32),
            pltpu.VMEM((steps, flat, TILE), F32),
            pltpu.VMEM((flat, TILE), F32),
            pltpu.VMEM((BAND, Y_LOW, X_CHIPS, piece, rows), BF16),
            pltpu.VMEM((BAND, X_CHIPS - 1, Y_LOW, piece, rows), BF16),
            pltpu.VMEM((BAND, X_CHIPS, piece, rows), BF16),
            pltpu.VMEM((BAND, piece, rows), BF16),
            pltpu.VMEM((piece, rows), F32),
            pltpu.VMEM((BAND, X_CHIPS, piece, rows), BF16),
            pltpu.VMEM((BAND, piece, rows), BF16),
            pltpu.VMEM((piece, rows), F32),
            pltpu.VMEM((BAND, X_CHIPS - 1, piece, rows), BF16),
            pltpu.VMEM((X_CHIPS, piece, rows), BF16),
            pltpu.VMEM((BAND, piece, rows), F32),
            pltpu.VMEM((piece, rows), F32),
            pltpu.VMEM((piece, rows), F32),
            dma((steps,)), dma((steps,)), dma,
            dma((4, 2, steps)), dma((4, 2, steps)),
            dma((steps, 3)), dma((steps, 3)), dma((steps, 3)), dma((steps, 3)),
            dma((3, steps)), dma((3, steps)),
            dma((BAND, 3)), dma((BAND, 3)), dma((BAND, 4)), dma((BAND, 4)),
        ],
        compiler_params=pltpu.CompilerParams(
            collective_id=0, has_side_effects=True, vmem_limit_bytes=56 << 20
        ),
        name="xc_matrix",
    )(
        basis_values, density, screen, atom_of_block, atom_factor,
        quad_weight.reshape(-1, TILE), core_density.reshape(-1, TILE),
    )


def solution(mesh):
    in_specs = (
        P(None, "row", "col"),
        P("row", None),
        P("row", "col"),
        P("col"),
        P(),
        P("col"),
        P("col"),
    )
    out_specs = P(("row", "col"), None)
    return jax.shard_map(body, mesh=mesh, in_specs=in_specs, out_specs=out_specs, check_vma=False)
```
